256 devices in a mesh: grp: 8 (over z), var: 32 (over x, y, core).
Axes of the slice: x: 4, y: 4, z: 8, core: 2. Of those that a mesh axis runs over, the one named last changes fastest.
Arguments:
- series: bfloat16 [8, 2048, 64, 128], P('grp', 'var'), parts along dimension 0, may hold values from -12 to 12
- sensor_total_count: int32 [8], P('grp'), parts along dimension 0, may hold values from 1024 to 2048
- depthwise_weight: bfloat16 [2048, 64, 51], P('var'), may hold values from -0.875 to 0.875
- batchnorm_gain: float32 [64], replicated, may hold values from 0.5 to 1.5
- batchnorm_bias: float32 [64], replicated, may hold values from -2 to 2
- channel_up_weight: bfloat16 [2048, 64, 256], P('var'), may hold values from -0.75 to 0.75
- channel_down_weight: bfloat16 [2048, 256, 64], P('var'), may hold values from -0.375 to 0.375
- down_factor1: bfloat16 [64, 8], replicated, may hold values from -0.75 to 0.75
- up_factor1: bfloat16 [8, 256], replicated, may hold values from -2 to 2
- sensor_up_weight: bfloat16 [64, 2048, 256], P('var'), may hold values from -0.125 to 0.125
- sensor_down_weight: bfloat16 [64, 256, 2048], P('var'), may hold values from -0.375 to 0.375
- down_factor2: bfloat16 [2048, 8], replicated, may hold values from -0.125 to 0.125
- up_factor2: bfloat16 [8, 256], replicated, may hold values from -2 to 2
- upstream: bfloat16 [8, 2048, 64, 128], P('grp', 'var'), parts along dimension 0, may hold values from -0.01171875 to 0.01171875
Outputs:
- mixed: bfloat16 [8, 2048, 64, 128], P('grp', 'var'), parts along dimension 0
- gradient_down_factor1: float32 [512, 8], P('grp'), parts along dimension 0
- gradient_up_factor1: float32 [64, 256], P('grp'), parts along dimension 0
- gradient_down_factor2: float32 [16384, 8], P('grp'), parts along dimension 0
- gradient_up_factor2: float32 [64, 256], P('grp'), parts along dimension 0
The draws below stay inside these ranges and needn't reach their ends.
There are 8 independent parts, one for each index of `grp`. The reference program is written for one: setup_inputs(seed, part) draws one part's arguments, and reference() takes and returns one part's arrays. A program takes and returns all parts, laid end to end along the dimension named above; an argument that names none is the same for every part. Nothing has to cross between parts.
All inputs are finite; a program needn't handle non-finite values.
Results may differ from the reference program's by a relative error of at most 0.028.
Values may be sent and summed in bfloat16 or wider, within the bound.
A program may use at most 128 MiB of HBM per device.

```python
import jax
import jax.numpy as jnp
from jax import lax

B = 1
SENSOR_SLOTS = 2048
CHANNEL_WIDTH = 64
N = 128
K = 51
CHANNEL_HIDDEN_1 = 256
SENSOR_HIDDEN_2 = 256
ADAPTER_RANK = 8


def draw_series(key, part):
    base_key, scale_key, shift_key = jax.random.split(key, 3)
    position = jnp.arange(SENSOR_SLOTS, dtype=jnp.float32) / SENSOR_SLOTS
    rough = jax.random.uniform(scale_key, (1, SENSOR_SLOTS, CHANNEL_WIDTH, 1), minval=0.6, maxval=1.4)
    noise = jax.random.normal(base_key, (B, SENSOR_SLOTS, CHANNEL_WIDTH, N))
    scales = 0.5 * 4.0 ** position
    offset = 0.4 * jax.random.normal(shift_key, (1, SENSOR_SLOTS, CHANNEL_WIDTH, 1))
    values = noise * scales[None, :, None, None] * rough + offset
    return jnp.clip(values, -12.0, 12.0).astype(jnp.bfloat16)


def block_scale(key, shape, cuts, smallest, high):
    gain = 1.0
    for dim, blocks in cuts:
        draws = jax.random.uniform(jax.random.fold_in(jax.random.fold_in(key, 6), dim), (blocks,), jnp.float32, smallest / len(cuts), high / len(cuts))
        gain = gain * jnp.repeat(jnp.exp(draws), shape[dim] // blocks).reshape((-1,) + (1,) * (len(shape) - 1 - dim))
    return gain


def bell_draw(stream_key, shape, deviation, reach, cuts=(), kind=jnp.bfloat16):
    array = jax.random.normal(stream_key, shape, jnp.float32) * deviation
    if len(cuts) > 0:
        array = block_scale(stream_key, shape, cuts, -0.22, 0.18) * array
    return jnp.clip(array, min=-reach, max=reach).astype(kind)


def setup_inputs(seed: int = 0, part: int = 0) -> dict:
    key_list = jax.random.split(jax.random.key(seed), 15)
    part_splits = jax.random.split(jax.random.fold_in(key_list[14], part), 15)
    series = draw_series(jax.random.fold_in(jax.random.fold_in(key_list[14], part), 71), part)
    sensor_total_count = jax.random.randint(part_splits[1], (1,), SENSOR_SLOTS // 2, SENSOR_SLOTS + 1).astype(jnp.int32)
    depthwise_weight = bell_draw(key_list[2], (SENSOR_SLOTS, CHANNEL_WIDTH, K), K ** -0.5, 0.875, ((0, 32),))
    batchnorm_gain = jnp.clip(jax.random.uniform(key_list[3], (CHANNEL_WIDTH,), jnp.float32, 0.5, 1.5), 0.5, 1.5)
    batchnorm_bias = bell_draw(key_list[4], (CHANNEL_WIDTH,), 0.5, 2.0, (), jnp.float32)
    channel_up_weight = bell_draw(key_list[5], (SENSOR_SLOTS, CHANNEL_WIDTH, CHANNEL_HIDDEN_1), CHANNEL_WIDTH ** -0.5, 0.75, ((0, 32),))
    channel_down_weight = bell_draw(key_list[6], (SENSOR_SLOTS, CHANNEL_HIDDEN_1, CHANNEL_WIDTH), CHANNEL_HIDDEN_1 ** -0.5, 0.375, ((0, 32),))
    down_factor1 = bell_draw(key_list[7], (CHANNEL_WIDTH, ADAPTER_RANK), CHANNEL_WIDTH ** -0.5, 0.75)
    up_factor1 = bell_draw(key_list[8], (ADAPTER_RANK, CHANNEL_HIDDEN_1), ADAPTER_RANK ** -0.5, 2.0)
    sensor_up_weight = bell_draw(key_list[9], (CHANNEL_WIDTH, SENSOR_SLOTS, SENSOR_HIDDEN_2), SENSOR_SLOTS ** -0.5, 0.125, ((0, 32),))
    sensor_down_weight = bell_draw(key_list[10], (CHANNEL_WIDTH, SENSOR_HIDDEN_2, SENSOR_SLOTS), SENSOR_HIDDEN_2 ** -0.5, 0.375, ((0, 32),))
    down_factor2 = bell_draw(key_list[11], (SENSOR_SLOTS, ADAPTER_RANK), SENSOR_SLOTS ** -0.5, 0.125)
    up_factor2 = bell_draw(key_list[12], (ADAPTER_RANK, SENSOR_HIDDEN_2), ADAPTER_RANK ** -0.5, 2.0)
    upstream = bell_draw(part_splits[13], (B, SENSOR_SLOTS, CHANNEL_WIDTH, N), (B * N * SENSOR_SLOTS) ** -0.5, 0.01171875, ((1, 32),))
    return dict(series=series, sensor_total_count=sensor_total_count, depthwise_weight=depthwise_weight, batchnorm_gain=batchnorm_gain, batchnorm_bias=batchnorm_bias, channel_up_weight=channel_up_weight, channel_down_weight=channel_down_weight, down_factor1=down_factor1, up_factor1=up_factor1, sensor_up_weight=sensor_up_weight, sensor_down_weight=sensor_down_weight, down_factor2=down_factor2, up_factor2=up_factor2, upstream=upstream)


tanh_scale = 0.7978845608028654
cubic_term = 0.044715

def gelu_value(values):
    return 0.5 * values * (1.0 + jnp.tanh(tanh_scale * (values + cubic_term * values * values * values)))

def gelu_slope(values):
    inner = jnp.tanh(tanh_scale * (values + cubic_term * values * values * values))
    return 0.5 * (1.0 + inner) + 0.5 * values * (1.0 - inner * inner) * tanh_scale * (1.0 + 3.0 * cubic_term * values * values)

def rounded_output(values):
    return lax.optimization_barrier(values.astype(jnp.bfloat16)).astype(jnp.float32)

def depthwise(series, depthwise_weight):
    patches = series.shape[-1]
    tap_count = depthwise_weight.shape[-1]
    half_width = tap_count // 2
    padded = jnp.pad(series.astype(jnp.float32), ((0, 0), (0, 0), (0, 0), (half_width, half_width)))
    kernel = depthwise_weight.astype(jnp.float32)
    total = jnp.zeros(series.shape, jnp.float32)
    for offset in range(tap_count):
        total = total + kernel[None, :, :, offset:offset + 1] * padded[:, :, :, offset:offset + patches]
    return total

def reference(series, sensor_total_count, depthwise_weight, batchnorm_gain, batchnorm_bias, channel_up_weight, channel_down_weight, down_factor1, up_factor1, sensor_up_weight, sensor_down_weight, down_factor2, up_factor2, upstream):
    live_limit = sensor_total_count[0]
    live_vec = (jnp.arange(SENSOR_SLOTS, dtype=jnp.int32) < live_limit).astype(jnp.float32)
    live_mask = live_vec[None, :, None, None]
    live_total = live_limit.astype(jnp.float32) * (B * N)
    convolved = depthwise(series, depthwise_weight)
    bn_mean = lax.optimization_barrier(jnp.sum(convolved * live_mask, axis=(0, 1, 3))) / live_total
    centered = convolved - bn_mean[None, None, :, None]
    spread = lax.optimization_barrier(jnp.sum(centered * centered * live_mask, axis=(0, 1, 3))) / live_total
    bn_scale = batchnorm_gain * lax.rsqrt(spread + 1e-05)
    normalized_rows = rounded_output((centered * bn_scale[None, None, :, None] + batchnorm_bias[None, None, :, None]) * live_mask)
    channel_up_weight32 = channel_up_weight.astype(jnp.float32)
    channel_down_weight32 = channel_down_weight.astype(jnp.float32)
    down_factor1_32 = down_factor1.astype(jnp.float32)
    up_factor1_32 = up_factor1.astype(jnp.float32)
    sensor_up_weight32 = sensor_up_weight.astype(jnp.float32)
    down_two32 = sensor_down_weight.astype(jnp.float32)
    down_factor2_32 = down_factor2.astype(jnp.float32)
    up_factor2_32 = up_factor2.astype(jnp.float32)
    first_rank_projection = rounded_output(jnp.einsum('tkie,if->tkfe', normalized_rows, down_factor1_32))
    first_preactivation = jnp.einsum('wlqk,lqz->wlzk', normalized_rows, channel_up_weight32) + jnp.einsum('pkui,uv->pkvi', first_rank_projection, up_factor1_32)
    first_hidden_state = rounded_output(gelu_value(first_preactivation))
    input_rows = rounded_output(jnp.einsum('uweg,wel->uwlg', first_hidden_state, channel_down_weight32))
    second_rank_projection = rounded_output(jnp.einsum('zjol,jy->zoly', input_rows, down_factor2_32))
    second_preactivation = jnp.einsum('pfyr,yfe->pyre', input_rows, sensor_up_weight32) + jnp.einsum('iezo,ot->iezt', second_rank_projection, up_factor2_32)
    hidden_two = rounded_output(gelu_value(second_preactivation))
    mixed_two = rounded_output(jnp.einsum('bdnj,djm->bmdn', hidden_two, down_two32))
    mixed = (series.astype(jnp.float32) + live_mask * mixed_two).astype(jnp.bfloat16)
    masked_up = upstream.astype(jnp.float32) * live_mask
    grad_hidden_two = jnp.einsum('bmdn,djm->bdnj', masked_up, down_two32)
    second_preactivation_gradient = rounded_output(grad_hidden_two * gelu_slope(second_preactivation))
    backward_second = rounded_output(jnp.einsum('gywi,xi->gywx', second_preactivation_gradient, up_factor2_32))
    gradient_up_factor2 = jnp.einsum('lghw,lghy->wy', second_rank_projection, second_preactivation_gradient)
    gradient_down_factor2 = jnp.einsum('oiux,ouxl->il', input_rows, backward_second)
    input_gradient = rounded_output(jnp.einsum('whgl,htl->wthg', second_preactivation_gradient, sensor_up_weight32) + jnp.einsum('apej,kj->akpe', backward_second, down_factor2_32))
    first_hidden_gradient = jnp.einsum('zyof,ylo->zylf', input_gradient, channel_down_weight32)
    first_preactivation_gradient = rounded_output(first_hidden_gradient * gelu_slope(first_preactivation))
    gradient_up_factor1 = jnp.einsum('udls,udks->lk', first_rank_projection, first_preactivation_gradient)
    backward_first = rounded_output(jnp.einsum('otzf,gz->otgf', first_preactivation_gradient, up_factor1_32))
    gradient_down_factor1 = jnp.einsum('cvsw,cvow->so', normalized_rows, backward_first)
    return (mixed, gradient_down_factor1, gradient_up_factor1, gradient_down_factor2, gradient_up_factor2)
```

```python
import jax
import jax.numpy as jnp
from jax import lax
from jax.experimental import pallas as pl
from jax.experimental.pallas import tpu as pltpu
from jax.sharding import PartitionSpec as P

F32 = jnp.float32
BF16 = jnp.bfloat16
MESH = pl.DeviceIdType.MESH

tanh_scale = 0.7978845608028654
cubic_term = 0.044715

PEERS = 32
SENSORS = 64
CHANNELS = 64
PATCHES = 128
TAPS = 51
HALF = TAPS // 2
GROUPS = 4
PADDED = PATCHES + 2 * HALF
SLOTS = PEERS * SENSORS
HIDDEN = 256
OWN = 2
CHUNKS = 2
CHUNK = SENSORS // CHUNKS
BLOCK = 16


def gelu_parts(v):
    square = v * v
    half = 0.5 * jnp.tanh(v * (tanh_scale + (tanh_scale * cubic_term) * square)) + 0.5
    value = v * half
    slope = half + (value * (1.0 - half)) * (
        2.0 * tanh_scale + (6.0 * tanh_scale * cubic_term) * square
    )
    return value, slope


def dot(a, b, contract=((1,), (0,))):
    return lax.dot_general(a, b, (contract, ((), ())), preferred_element_type=F32)


NT = ((1,), (1,))
TN = ((0,), (0,))


def offset_peer(me, offset, sign):
    x, y, c = me // 8, (me // 2) % 4, me % 2
    dx, dy, dc = offset // 8, (offset // 2) % 4, offset % 2
    return (
        ((x + 4 + sign * dx) % 4) * 8 + ((y + 4 + sign * dy) % 4) * 2 + (c + 2 + sign * dc) % 2
    )


def offset_of(me, peer):
    dx = (peer // 8 + 4 - me // 8) % 4
    dy = ((peer // 2) % 4 + 4 - (me // 2) % 4) % 4
    dc = (peer % 2 + 2 - me % 2) % 2
    return dx * 8 + dy * 2 + dc


def kernel(
    count_ref,
    gain_ref,
    bias_ref,
    df1_ref,
    uf1_ref,
    df2_ref,
    uf2_ref,
    series_hbm,
    taps_hbm,
    up1_hbm,
    down1_hbm,
    up2_hbm,
    down2_hbm,
    upstream_hbm,
    mixed_hbm,
    gd1_ref,
    gu1_ref,
    gd2_ref,
    gu2_ref,
    series,
    taps,
    up1,
    down1,
    up2,
    down2,
    upstream,
    padded,
    packed_taps,
    conv,
    rows32,
    normed_ref,
    low_t,
    slope_ref,
    u_send,
    u_recv,
    f_send,
    f_recv,
    g_send,
    g_recv,
    m_send,
    m_recv,
    out_buf,
    st_send,
    st_recv,
    dft,
    ufr,
    gh_ref,
    hid_ref,
    gp2_ref,
    back_ref,
    part,
    part_recv,
    total,
    total_recv,
    load_sems,
    self_sems,
    u_ssem,
    u_rsem,
    st_ssem,
    st_rsem,
    f_ssem,
    f_rsem,
    g_ssem,
    g_rsem,
    m_ssem,
    m_rsem,
    p_ssem,
    p_rsem,
    t_ssem,
    t_rsem,
):
    me = lax.axis_index("var")
    limit = count_ref[0]
    live_rows = limit - me * SENSORS

    def remote(src, dst, ssem, rsem, peer):
        return pltpu.make_async_remote_copy(
            src_ref=src,
            dst_ref=dst,
            send_sem=ssem,
            recv_sem=rsem,
            device_id={"var": peer},
            device_id_type=MESH,
        )

    loads = [
        pltpu.make_async_copy(src, dst, load_sems.at[i])
        for i, (src, dst) in enumerate(
            (
                (upstream_hbm, upstream),
                (series_hbm, series),
                (taps_hbm, taps),
                (up1_hbm, up1),
                (down1_hbm, down1),
                (down2_hbm, down2),
                (up2_hbm, up2),
            )
        )
    ]
    for load in loads:
        load.start()

    barrier = pltpu.get_barrier_semaphore()

    @pl.loop(1, PEERS)
    def _(o):
        pl.semaphore_signal(
            barrier, inc=1, device_id={"var": offset_peer(me, o, 1)}, device_id_type=MESH
        )

    loads[0].wait()
    row_index = lax.broadcasted_iota(jnp.int32, (SENSORS, PATCHES), 0)
    live_sensor = (row_index < live_rows).astype(F32)

    @pl.loop(0, SENSORS)
    def _(m):
        rows32[pl.ds(m, CHANNELS, stride=SENSORS), :] = upstream[m].astype(F32)

    @pl.loop(0, CHANNELS)
    def _(d):
        at = pl.multiple_of(d * SENSORS, SENSORS)
        u_send[d] = (rows32[pl.ds(at, SENSORS), :] * live_sensor).astype(BF16)

    pl.semaphore_wait(barrier, PEERS - 1)
    mine = pl.ds(pl.multiple_of(me * SENSORS, SENSORS), SENSORS)

    def u_copy(o, peer):
        return remote(
            u_send.at[pl.ds(OWN * peer, OWN)],
            u_recv.at[:, mine, :],
            u_ssem.at[o],
            u_rsem.at[o],
            peer,
        )

    @pl.loop(1, PEERS)
    def _(o):
        u_copy(o, offset_peer(me, o, 1)).start()

    u_self = pltpu.make_async_copy(
        u_send.at[pl.ds(OWN * me, OWN)], u_recv.at[:, mine, :], self_sems.at[0]
    )
    u_self.start()

    df1 = df1_ref[...].astype(F32)
    zero8 = jnp.zeros((8, CHANNELS), F32)
    dft[...] = jnp.concatenate(
        [
            jnp.concatenate([df1, zero8], axis=1),
            jnp.concatenate([zero8, df1], axis=1),
            jnp.zeros((112, 128), F32),
        ],
        axis=0,
    ).astype(BF16)
    uf1_32 = uf1_ref[...].astype(F32)
    ufr[0] = jnp.concatenate([uf1_32, jnp.zeros((120, HIDDEN), F32)], axis=0).astype(BF16)
    ufr[1] = jnp.concatenate(
        [jnp.zeros((8, HIDDEN), F32), uf1_32, jnp.zeros((112, HIDDEN), F32)], axis=0
    ).astype(BF16)

    loads[1].wait()
    loads[2].wait()
    padded[:, 0 : HALF * 8, :] = jnp.zeros((GROUPS, HALF * 8, 128), F32)
    padded[:, (HALF + PATCHES) * 8 : PADDED * 8, :] = jnp.zeros((GROUPS, HALF * 8, 128), F32)

    for g in range(GROUPS):

        @pl.loop(0, 8)
        def _(r):
            both = jnp.concatenate(
                [series[16 * g + r].astype(F32), series[16 * g + 8 + r].astype(F32)], axis=0
            )
            padded[g, pl.ds(HALF * 8 + r, PATCHES, stride=8), :] = both.T

    @pl.loop(0, TAPS)
    def _(k):
        row = taps[k].astype(F32)
        for g in range(GROUPS):
            packed_taps[k, g] = jnp.concatenate(
                [row[16 * g : 16 * g + 8], row[16 * g + 8 : 16 * g + 16]], axis=1
            )

    sub = lax.broadcasted_iota(jnp.int32, (8, 128), 0)
    lane = lax.broadcasted_iota(jnp.int32, (8, 128), 1)
    high = (lane >= CHANNELS).astype(jnp.int32) * 8

    def group_mask(g):
        return (sub + high + 16 * g < live_rows).astype(F32)

    def conv_group(g, sums):
        def conv_block(nb, acc_sum):
            base = pl.multiple_of(nb * (BLOCK * 8), BLOCK * 8)
            acc = [None] * BLOCK
            tap = {}
            for j in range(BLOCK + TAPS - 1):
                x = padded[g, pl.ds(base + 8 * j, 8), :]
                if j < TAPS:
                    tap[j] = packed_taps[j, g]
                for i in range(max(0, j - TAPS + 1), min(BLOCK - 1, j) + 1):
                    term = tap[j - i] * x
                    acc[i] = term if acc[i] is None else acc[i] + term
            for i in range(BLOCK):
                conv[g, pl.ds(base + 8 * i, 8), :] = acc[i]
                acc_sum = acc_sum + acc[i]
            return acc_sum

        group_sum = lax.fori_loop(0, PATCHES // BLOCK, conv_block, jnp.zeros((8, 128), F32))
        return sums + group_sum * group_mask(g)

    sums = lax.fori_loop(0, GROUPS, conv_group, jnp.zeros((8, 128), F32))

    def fold(v):
        v = jnp.sum(v, axis=0, keepdims=True)
        return v + pltpu.roll(v, CHANNELS, axis=1)

    sum_row = fold(sums)
    own_count = jnp.clip(live_rows, 0, SENSORS).astype(F32) * PATCHES
    own_mean = sum_row / jnp.maximum(own_count, 1.0)

    def square_group(g, squares):
        def block(b, acc):
            at = pl.multiple_of(b * 128, 128)
            c = conv[g, pl.ds(at, 128), :] - own_mean
            return acc + jnp.sum((c * c).reshape(16, 8, 128), axis=0)

        group = lax.fori_loop(0, 8, block, jnp.zeros((8, 128), F32))
        return squares + group * group_mask(g)

    square_row = fold(lax.fori_loop(0, GROUPS, square_group, jnp.zeros((8, 128), F32)))
    stats = jnp.where(
        sub == 0,
        sum_row,
        jnp.where(sub == 1, square_row, jnp.where(sub == 2, own_mean, own_count)),
    )
    st_send[...] = stats
    st_recv[me] = stats

    def st_copy(o, peer):
        return remote(st_send, st_recv.at[me], st_ssem.at[o], st_rsem.at[o], peer)

    @pl.loop(1, PEERS)
    def _(o):
        st_copy(o, offset_peer(me, o, 1)).start()

    @pl.loop(1, PEERS)
    def _(o):
        st_copy(o, offset_peer(me, o, 1)).wait()

    st_all = st_recv[...]
    st_sum = jnp.sum(st_all, axis=0)
    live_total = limit.astype(F32) * PATCHES
    bn_mean = st_sum[0:1] / live_total
    means = st_all[:, 2:3, :] - bn_mean[None]
    shift_squares = jnp.sum(st_all[:, 3:4, :] * means * means, axis=0)
    spread = (st_sum[1:2] + shift_squares) / live_total
    gain = jnp.concatenate([gain_ref[...], gain_ref[...]], axis=1)
    bias = jnp.concatenate([bias_ref[...], bias_ref[...]], axis=1)
    bn_scale = gain * lax.rsqrt(spread + 1e-05)

    loads[3].wait()
    loads[4].wait()
    zero_half = jnp.zeros((CHANNELS, HIDDEN), BF16)
    lane_row = lax.broadcasted_iota(jnp.int32, (1, 128), 1)
    high_row = (lane_row >= CHANNELS).astype(jnp.int32) * 8

    def f_copy(c, o, peer):
        return remote(
            f_send.at[c, pl.ds(OWN * peer, OWN)],
            f_recv.at[:, pl.ds(pl.multiple_of(me * SENSORS + c * CHUNK, CHUNK), CHUNK), :],
            f_ssem.at[c * PEERS + o],
            f_rsem.at[c * PEERS + o],
            peer,
        )

    f_self = []
    for c in range(CHUNKS):
        for gl in range(GROUPS // CHUNKS):
            g = c * (GROUPS // CHUNKS) + gl

            @pl.loop(0, 8)
            def _(r):
                pair = g * 8 + r
                live = (high_row + 16 * g + r < live_rows).astype(F32)
                centered = conv[g, pl.ds(r, PATCHES, stride=8), :] - bn_mean
                normed = ((centered * bn_scale + bias) * live).astype(BF16)
                normed_ref[pair] = normed
                low = dot(normed, dft[...], NT).astype(BF16)
                low_t[pair] = dot(dft[0:16, :], normed, NT).astype(BF16)
                lhs = jnp.concatenate([normed, low], axis=1)
                for half in range(2):
                    m = 16 * g + 8 * half + r
                    weight = up1[m]
                    rhs = jnp.concatenate(
                        [weight, zero_half, ufr[half]] if half == 0 else [zero_half, weight, ufr[half]],
                        axis=0,
                    )
                    value, slope = gelu_parts(dot(lhs, rhs))
                    slope_ref[m] = slope
                    feature = dot(down1[m], value.astype(BF16), NT)
                    rows32[pl.ds(16 * gl + 8 * half + r, CHANNELS, stride=CHUNK), :] = feature

        @pl.loop(0, CHANNELS)
        def _(d):
            at = pl.multiple_of(d * CHUNK, CHUNK)
            f_send[c, d] = rows32[pl.ds(at, CHUNK), :].astype(BF16)

        @pl.loop(1, PEERS)
        def _(o):
            f_copy(c, o, offset_peer(me, o, 1)).start()

        f_self.append(
            pltpu.make_async_copy(
                f_send.at[c, pl.ds(OWN * me, OWN)],
                f_recv.at[:, pl.ds(pl.multiple_of(me * SENSORS + c * CHUNK, CHUNK), CHUNK), :],
                self_sems.at[1 + c],
            )
        )
        f_self[-1].start()

    u_self.wait()

    @pl.loop(1, PEERS)
    def _(o):
        u_copy(o, offset_peer(me, o, 1)).wait()

    loads[5].wait()
    loads[6].wait()
    for dd in range(OWN):
        gh_ref[dd] = dot(down2[dd], u_recv[dd]).T

    for c in range(CHUNKS):
        f_self[c].wait()

        @pl.loop(1, PEERS)
        def _(o):
            f_copy(c, o, offset_peer(me, o, 1)).wait()

    for dd in range(OWN):

        def mix(b, carry):
            pre, low = carry
            at = pl.ds(pl.multiple_of(b * 256, 256), 256)
            f = f_recv[dd, at, :]
            return pre + dot(f, up2[dd, at, :], TN), low + dot(df2_ref[:, at], f)

        pre, low = lax.fori_loop(
            0,
            SLOTS // 256,
            mix,
            (jnp.zeros((PATCHES, HIDDEN), F32), jnp.zeros((8, PATCHES), F32)),
        )
        low = low.astype(BF16)
        value, slope = gelu_parts(pre + dot(low, uf2_ref[...], TN))
        hid_ref[dd] = value.astype(BF16)
        gp2 = (gh_ref[dd] * slope).astype(BF16)
        gp2_ref[dd] = gp2
        back_ref[dd] = dot(uf2_ref[...], gp2, NT).astype(BF16)
        gu2 = dot(low, gp2)
        for t in range(2):
            tile = gu2[:, 128 * t : 128 * (t + 1)]
            part[16 + t] = tile if dd == 0 else part[16 + t] + tile

    own_block = pl.ds(OWN * me, OWN)

    def g_copy(peer):
        o = offset_of(me, peer)
        return remote(g_send.at[peer], g_recv.at[own_block], g_ssem.at[o], g_rsem.at[o], peer)

    def m_copy(peer):
        o = offset_of(me, peer)
        return remote(m_send.at[peer], m_recv.at[own_block], m_ssem.at[o], m_rsem.at[o], peer)

    def send_both(copy, sender, receiver, sem, chip):
        for core in range(2):
            peer = 2 * chip + core

            @pl.when(peer != me)
            def _():
                copy(peer).start()

            @pl.when(peer == me)
            def _():
                pltpu.make_async_copy(sender.at[peer], receiver.at[own_block], sem).start()

    @pl.loop(1, 17)
    def _(i):
        chip = offset_peer(me, 2 * (i % 16), 1) // 2
        at = pl.ds(pl.multiple_of(chip * 128, 128), 128)
        gd2 = jnp.zeros((8, 128), F32)
        for dd in range(OWN):
            grad = dot(up2[dd, at, :], gp2_ref[dd], NT) + dot(df2_ref[:, at], back_ref[dd], TN)
            gd2 = gd2 + dot(back_ref[dd], f_recv[dd, at, :], NT)
            grad = grad.astype(BF16)
            g_send[2 * chip, dd] = grad[0:SENSORS]
            g_send[2 * chip + 1, dd] = grad[SENSORS:]
        part[chip] = gd2
        send_both(g_copy, g_send, g_recv, self_sems.at[3], chip)

    @pl.loop(1, 17)
    def _(i):
        chip = offset_peer(me, 2 * (i % 16), 1) // 2
        at = pl.ds(pl.multiple_of(chip * 128, 128), 128)
        for dd in range(OWN):
            mix_t = dot(hid_ref[dd], down2[dd, :, at]).T.astype(BF16)
            m_send[2 * chip, dd] = mix_t[0:SENSORS]
            m_send[2 * chip + 1, dd] = mix_t[SENSORS:]
        send_both(m_copy, m_send, m_recv, self_sems.at[4], chip)

    def self_wait(sender, receiver, sem):
        pltpu.make_async_copy(sender.at[me], receiver.at[own_block], sem).wait()

    self_wait(g_send, g_recv, self_sems.at[3])

    @pl.loop(1, PEERS)
    def _(o):
        g_copy(offset_peer(me, o, 1)).wait()

    @pl.loop(0, CHANNELS)
    def _(d):
        at = pl.multiple_of(d * SENSORS, SENSORS)
        rows32[pl.ds(at, SENSORS), :] = g_recv[d].astype(F32)

    gu1 = jnp.zeros((8, HIDDEN), F32)
    gd1 = jnp.zeros((16, 128), F32)
    for g in range(GROUPS):

        def back(r, carry):
            gu1, gd1 = carry
            pair = g * 8 + r
            grad = jnp.concatenate(
                [
                    rows32[pl.ds(16 * g + 8 * half + r, CHANNELS, stride=SENSORS), :]
                    for half in range(2)
                ],
                axis=0,
            ).T.astype(BF16)
            gps, backs = [], []
            for half in range(2):
                m = 16 * g + 8 * half + r
                weight = down1[m]
                rhs = jnp.concatenate(
                    [weight, zero_half] if half == 0 else [zero_half, weight], axis=0
                )
                gp = (dot(grad, rhs) * slope_ref[m]).astype(BF16)
                gps.append(gp)
                backs.append(dot(uf1_ref[...], gp, NT))
            low = low_t[pair].astype(F32)
            lhs = jnp.concatenate([low[0:8], low[8:16]], axis=1).astype(BF16)
            gu1 = gu1 + dot(lhs, jnp.concatenate(gps, axis=0))
            gd1 = gd1 + dot(jnp.concatenate(backs, axis=0).astype(BF16), normed_ref[pair])
            return gu1, gd1

        gu1, gd1 = lax.fori_loop(0, 8, back, (gu1, gd1))

    part[18] = gu1[:, 0:128]
    part[19] = gu1[:, 128:256]
    part[20] = jnp.where(lane < CHANNELS, gd1[0:8], gd1[8:16])

    TILES = 21
    part_recv[me] = part[jnp.minimum(me, TILES - 1)]

    def p_copy(tile, o):
        return remote(part.at[tile], part_recv.at[me], p_ssem.at[o], p_rsem.at[o], tile)

    @pl.loop(1, PEERS)
    def _(o):
        peer = offset_peer(me, o, 1)

        @pl.when(peer < TILES)
        def _():
            p_copy(peer, o).start()

    def t_copy(peer, o):
        return remote(total, total_recv.at[me], t_ssem.at[o], t_rsem.at[o], peer)

    @pl.when(me < TILES)
    def _():
        @pl.loop(1, PEERS)
        def _(o):
            p_copy(me, o).wait_recv()

        summed = jnp.sum(part_recv[...], axis=0)
        total[...] = summed
        total_recv[me] = summed

        @pl.loop(1, PEERS)
        def _(o):
            t_copy(offset_peer(me, o, 1), o).start()

    @pl.loop(1, PEERS)
    def _(o):
        source = offset_peer(me, o, -1)

        @pl.when(source < TILES)
        def _():
            t_copy(source, o).wait_recv()

    for t in range(16):
        gd2_ref[:, 128 * t : 128 * (t + 1)] = total_recv[t]
    for t in range(2):
        gu2_ref[:, 128 * t : 128 * (t + 1)] = total_recv[16 + t]
        gu1_ref[:, 128 * t : 128 * (t + 1)] = total_recv[18 + t]
    both = total_recv[20]
    gd1_ref[...] = (both + pltpu.roll(both, CHANNELS, axis=1))[:, 0:CHANNELS]

    self_wait(m_send, m_recv, self_sems.at[4])

    @pl.loop(1, PEERS)
    def _(o):
        m_copy(offset_peer(me, o, 1)).wait()

    @pl.loop(0, CHANNELS)
    def _(d):
        at = pl.multiple_of(d * SENSORS, SENSORS)
        rows32[pl.ds(at, SENSORS), :] = m_recv[d].astype(F32) * live_sensor

    @pl.loop(0, SENSORS)
    def _(m):
        out_buf[m] = (
            series[m].astype(F32) + rows32[pl.ds(m, CHANNELS, stride=SENSORS), :]
        ).astype(BF16)

    store = pltpu.make_async_copy(out_buf, mixed_hbm, load_sems.at[0])
    store.start()

    @pl.loop(1, PEERS)
    def _(o):
        peer = offset_peer(me, o, 1)

        @pl.when(peer < TILES)
        def _():
            p_copy(peer, o).wait_send()

        @pl.when(me < TILES)
        def _():
            t_copy(peer, o).wait_send()

    store.wait()


def body(
    series,
    sensor_total_count,
    depthwise_weight,
    batchnorm_gain,
    batchnorm_bias,
    channel_up_weight,
    channel_down_weight,
    down_factor1,
    up_factor1,
    sensor_up_weight,
    sensor_down_weight,
    down_factor2,
    up_factor2,
    upstream,
):
    vmem = pl.BlockSpec(memory_space=pltpu.VMEM)
    hbm = pl.BlockSpec(memory_space=pltpu.HBM)
    rows = PATCHES * 8
    dma = pltpu.SemaphoreType.DMA
    mixed, gd1, gu1, gd2, gu2 = pl.pallas_call(
        kernel,
        out_shape=(
            jax.ShapeDtypeStruct((SENSORS, CHANNELS, PATCHES), BF16),
            jax.ShapeDtypeStruct((8, CHANNELS), F32),
            jax.ShapeDtypeStruct((8, HIDDEN), F32),
            jax.ShapeDtypeStruct((8, SLOTS), F32),
            jax.ShapeDtypeStruct((8, HIDDEN), F32),
        ),
        in_specs=[pl.BlockSpec(memory_space=pltpu.SMEM)] + [vmem] * 6 + [hbm] * 7,
        out_specs=(hbm, vmem, vmem, vmem, vmem),
        scratch_shapes=[
            pltpu.VMEM((SENSORS, CHANNELS, PATCHES), BF16),
            pltpu.VMEM((TAPS, SENSORS, CHANNELS), BF16),
            pltpu.VMEM((SENSORS, CHANNELS, HIDDEN), BF16),
            pltpu.VMEM((SENSORS, CHANNELS, HIDDEN), BF16),
            pltpu.VMEM((OWN, SLOTS, HIDDEN), BF16),
            pltpu.VMEM((OWN, HIDDEN, SLOTS), BF16),
            pltpu.VMEM((SENSORS, CHANNELS, PATCHES), BF16),
            pltpu.VMEM((GROUPS, PADDED * 8, 128), F32),
            pltpu.VMEM((TAPS, GROUPS, 8, 128), F32),
            pltpu.VMEM((GROUPS, rows, 128), F32),
            pltpu.VMEM((SENSORS * CHANNELS, PATCHES), F32),
            pltpu.VMEM((SENSORS // 2, PATCHES, 128), BF16),
            pltpu.VMEM((SENSORS // 2, 16, PATCHES), BF16),
            pltpu.VMEM((SENSORS, PATCHES, HIDDEN), F32),
            pltpu.VMEM((CHANNELS, SENSORS, PATCHES), BF16),
            pltpu.VMEM((OWN, SLOTS, PATCHES), BF16),
            pltpu.VMEM((CHUNKS, CHANNELS, CHUNK, PATCHES), BF16),
            pltpu.VMEM((OWN, SLOTS, PATCHES), BF16),
            pltpu.VMEM((PEERS, OWN, SENSORS, PATCHES), BF16),
            pltpu.VMEM((CHANNELS, SENSORS, PATCHES), BF16),
            pltpu.VMEM((PEERS, OWN, SENSORS, PATCHES), BF16),
            pltpu.VMEM((CHANNELS, SENSORS, PATCHES), BF16),
            pltpu.VMEM((SENSORS, CHANNELS, PATCHES), BF16),
            pltpu.VMEM((8, 128), F32),
            pltpu.VMEM((PEERS, 8, 128), F32),
            pltpu.VMEM((128, 128), BF16),
            pltpu.VMEM((2, 128, HIDDEN), BF16),
            pltpu.VMEM((OWN, PATCHES, HIDDEN), F32),
            pltpu.VMEM((OWN, PATCHES, HIDDEN), BF16),
            pltpu.VMEM((OWN, PATCHES, HIDDEN), BF16),
            pltpu.VMEM((OWN, 8, PATCHES), BF16),
            pltpu.VMEM((PEERS, 8, 128), F32),
            pltpu.VMEM((PEERS, 8, 128), F32),
            pltpu.VMEM((8, 128), F32),
            pltpu.VMEM((PEERS, 8, 128), F32),
            dma((7,)),
            dma((5,)),
            dma((PEERS,)),
            dma((PEERS,)),
            dma((PEERS,)),
            dma((PEERS,)),
            dma((CHUNKS * PEERS,)),
            dma((CHUNKS * PEERS,)),
            dma((PEERS,)),
            dma((PEERS,)),
            dma((PEERS,)),
            dma((PEERS,)),
            dma((PEERS,)),
            dma((PEERS,)),
            dma((PEERS,)),
            dma((PEERS,)),
        ],
        compiler_params=pltpu.CompilerParams(
            collective_id=0, has_side_effects=True, vmem_limit_bytes=60 * 1024 * 1024
        ),
        cost_estimate=pl.CostEstimate(
            flops=2_000_000_000, bytes_accessed=12_000_000, transcendentals=2_200_000
        ),
    )(
        sensor_total_count,
        batchnorm_gain.reshape(1, CHANNELS),
        batchnorm_bias.reshape(1, CHANNELS),
        down_factor1.T,
        up_factor1,
        down_factor2.T,
        up_factor2,
        series[0],
        jnp.transpose(depthwise_weight, (2, 0, 1)),
        channel_up_weight,
        jnp.transpose(channel_down_weight, (0, 2, 1)),
        sensor_up_weight,
        sensor_down_weight,
        upstream[0],
    )
    return mixed[None], gd1.T, gu1, gd2.T, gu2


def solution(mesh):
    placed = (
        P("grp", "var", None, None),
        P("grp"),
        P("var", None, None),
        P(),
        P(),
        P("var", None, None),
        P("var", None, None),
        P(),
        P(),
        P("var", None, None),
        P("var", None, None),
        P(),
        P(),
        P("grp", "var", None, None),
    )
    return jax.shard_map(
        body,
        mesh=mesh,
        in_specs=placed,
        out_specs=(
            P("grp", "var", None, None),
            P("grp", None),
            P("grp", None),
            P("grp", None),
            P("grp", None),
        ),
        check_vma=False,
    )
```

```python
import jax
import jax.numpy as jnp
from jax import lax
from jax.experimental import pallas as pl
from jax.experimental.pallas import tpu as pltpu
from jax.sharding import PartitionSpec as P

F32 = jnp.float32
BF16 = jnp.bfloat16
MESH = pl.DeviceIdType.MESH

tanh_scale = 0.7978845608028654
cubic_term = 0.044715

PEERS = 32
SENSORS = 64
CHANNELS = 64
PATCHES = 128
TAPS = 51
HALF = TAPS // 2
GROUPS = 4
PADDED = PATCHES + 2 * HALF
SLOTS = PEERS * SENSORS
HIDDEN = 256
OWN = 2
CHUNKS = 4
CHUNK = SENSORS // CHUNKS
HALVES = 2
BATCH = SENSORS // HALVES
TILES = 21
STEP = 16
BLOCK = 16


def gelu_parts(v):
    square = v * v
    half = 0.5 * jnp.tanh(v * (tanh_scale + (tanh_scale * cubic_term) * square)) + 0.5
    value = v * half
    slope = half + (value * (1.0 - half)) * (
        2.0 * tanh_scale + (6.0 * tanh_scale * cubic_term) * square
    )
    return value, slope


def dot(a, b, contract=((1,), (0,))):
    return lax.dot_general(a, b, (contract, ((), ())), preferred_element_type=F32)


NT = ((1,), (1,))
TN = ((0,), (0,))


def offset_peer(me, offset, sign):
    x, y, c = me // 8, (me // 2) % 4, me % 2
    dx, dy, dc = offset // 8, (offset // 2) % 4, offset % 2
    return (
        ((x + 4 + sign * dx) % 4) * 8 + ((y + 4 + sign * dy) % 4) * 2 + (c + 2 + sign * dc) % 2
    )


def peer_at(me, i):
    return offset_peer(me, (i + 18) % (PEERS - 1) + 1, 1)


def kernel(
    count_ref,
    gain_ref,
    bias_ref,
    df1_ref,
    uf1_ref,
    df2_ref,
    uf2_ref,
    series_hbm,
    taps_hbm,
    up1_hbm,
    down1_hbm,
    up2_hbm,
    down2_hbm,
    upstream_hbm,
    m_recv,
    total_out,
    series,
    taps,
    up1,
    down1,
    up2,
    down2,
    upstream,
    padded,
    packed_taps,
    conv,
    rows32,
    normed_ref,
    low_t,
    slope_ref,
    u_send,
    u_recv,
    f_send,
    f_recv,
    g_send,
    g_recv,
    m_send,
    st_send,
    st_recv,
    dft,
    ufr,
    gh_ref,
    hid_ref,
    gp2_ref,
    back_ref,
    part,
    part_recv,
    total,
    total_recv,
    load_sems,
    self_sems,
    sends,
    arrivals,
):
    me = lax.axis_index("var")
    limit = count_ref[0]
    live_rows = limit - me * SENSORS

    def remote(src, dst, ssem, rsem, peer):
        return pltpu.make_async_remote_copy(
            src_ref=src,
            dst_ref=dst,
            send_sem=ssem,
            recv_sem=rsem,
            device_id={"var": peer},
            device_id_type=MESH,
        )

    loads = [
        pltpu.make_async_copy(src, dst, load_sems.at[i])
        for i, (src, dst) in enumerate(
            (
                (upstream_hbm, upstream),
                (series_hbm, series),
                (taps_hbm, taps),
                (up1_hbm, up1),
                (down1_hbm, down1),
                (down2_hbm, down2),
                (up2_hbm, up2),
            )
        )
    ]
    for load in loads:
        load.start()

    barrier = pltpu.get_barrier_semaphore()

    @pl.loop(1, PEERS)
    def _(o):
        pl.semaphore_signal(
            barrier, inc=1, device_id={"var": offset_peer(me, o, 1)}, device_id_type=MESH
        )

    loads[0].wait()
    row_index = lax.broadcasted_iota(jnp.int32, (SENSORS, PATCHES), 0)
    live_sensor = (row_index < live_rows).astype(F32)

    @pl.loop(0, SENSORS, unroll=8)
    def _(m):
        rows32[pl.ds(m, CHANNELS, stride=SENSORS), :] = upstream[m].astype(F32)

    @pl.loop(0, CHANNELS, unroll=8)
    def _(d):
        at = pl.multiple_of(d * SENSORS, SENSORS)
        u_send[d] = (rows32[pl.ds(at, SENSORS), :] * live_sensor).astype(BF16)

    pl.semaphore_wait(barrier, PEERS - 1)
    mine = pl.ds(pl.multiple_of(me * SENSORS, SENSORS), SENSORS)

    neighbour = offset_peer(me, 1, 1)

    @pl.loop(1, PEERS)
    def _(i):
        peer = peer_at(me, i)
        remote(
            u_send.at[pl.ds(OWN * peer, OWN)], u_recv.at[:, mine, :], sends.at[0], arrivals.at[0], peer
        ).start()

    u_self = pltpu.make_async_copy(
        u_send.at[pl.ds(OWN * me, OWN)], u_recv.at[:, mine, :], self_sems.at[0]
    )
    u_self.start()
    u_all = remote(
        u_send.at[pl.ds(0, OWN * (PEERS - 1))],
        u_recv.at[:, pl.ds(0, SENSORS * (PEERS - 1)), :],
        sends.at[0],
        arrivals.at[0],
        neighbour,
    )

    df1 = df1_ref[...].astype(F32)
    zero8 = jnp.zeros((8, CHANNELS), F32)
    dft[...] = jnp.concatenate(
        [
            jnp.concatenate([df1, zero8], axis=1),
            jnp.concatenate([zero8, df1], axis=1),
            jnp.zeros((112, 128), F32),
        ],
        axis=0,
    ).astype(BF16)
    uf1_32 = uf1_ref[...].astype(F32)
    ufr[0] = jnp.concatenate([uf1_32, jnp.zeros((120, HIDDEN), F32)], axis=0).astype(BF16)
    ufr[1] = jnp.concatenate(
        [jnp.zeros((8, HIDDEN), F32), uf1_32, jnp.zeros((112, HIDDEN), F32)], axis=0
    ).astype(BF16)

    loads[1].wait()
    loads[2].wait()
    padded[:, 0 : HALF * 8, :] = jnp.zeros((GROUPS, HALF * 8, 128), F32)
    padded[:, (HALF + PATCHES) * 8 : PADDED * 8, :] = jnp.zeros((GROUPS, HALF * 8, 128), F32)

    for g in range(GROUPS):

        @pl.loop(0, 8, unroll=4)
        def _(r):
            both = jnp.concatenate(
                [series[16 * g + r].astype(F32), series[16 * g + 8 + r].astype(F32)], axis=0
            )
            padded[g, pl.ds(HALF * 8 + r, PATCHES, stride=8), :] = both.T

    @pl.loop(0, TAPS, unroll=3)
    def _(k):
        row = taps[k].astype(F32)
        for g in range(GROUPS):
            packed_taps[k, g] = jnp.concatenate(
                [row[16 * g : 16 * g + 8], row[16 * g + 8 : 16 * g + 16]], axis=1
            )

    sub = lax.broadcasted_iota(jnp.int32, (8, 128), 0)
    lane = lax.broadcasted_iota(jnp.int32, (8, 128), 1)
    high = (lane >= CHANNELS).astype(jnp.int32) * 8

    def group_mask(g):
        return (sub + high + 16 * g < live_rows).astype(F32)

    def conv_group(g, sums):
        def conv_block(nb, acc_sum):
            base = pl.multiple_of(nb * (BLOCK * 8), BLOCK * 8)
            acc = [None] * BLOCK
            tap = {}
            for j in range(BLOCK + TAPS - 1):
                x = padded[g, pl.ds(base + 8 * j, 8), :]
                if j < TAPS:
                    tap[j] = packed_taps[j, g]
                for i in range(max(0, j - TAPS + 1), min(BLOCK - 1, j) + 1):
                    term = tap[j - i] * x
                    acc[i] = term if acc[i] is None else acc[i] + term
            for i in range(BLOCK):
                conv[g, pl.ds(base + 8 * i, 8), :] = acc[i]
                acc_sum = acc_sum + acc[i]
            return acc_sum

        group_sum = lax.fori_loop(0, PATCHES // BLOCK, conv_block, jnp.zeros((8, 128), F32))
        return sums + group_sum * group_mask(g)

    sums = lax.fori_loop(0, GROUPS, conv_group, jnp.zeros((8, 128), F32))

    def fold(v):
        v = jnp.sum(v, axis=0, keepdims=True)
        return v + pltpu.roll(v, CHANNELS, axis=1)

    sum_row = fold(sums)
    own_count = jnp.clip(live_rows, 0, SENSORS).astype(F32) * PATCHES
    own_mean = sum_row / jnp.maximum(own_count, 1.0)

    def square_group(g, squares):
        def block(b, acc):
            at = pl.multiple_of(b * 128, 128)
            c = conv[g, pl.ds(at, 128), :] - own_mean
            return acc + jnp.sum((c * c).reshape(16, 8, 128), axis=0)

        group = lax.fori_loop(0, 8, block, jnp.zeros((8, 128), F32))
        return squares + group * group_mask(g)

    square_row = fold(lax.fori_loop(0, GROUPS, square_group, jnp.zeros((8, 128), F32)))
    stats = jnp.where(
        sub == 0,
        sum_row,
        jnp.where(sub == 1, square_row, jnp.where(sub == 2, own_mean, own_count)),
    )
    st_send[...] = stats
    st_recv[me] = stats

    @pl.loop(1, PEERS)
    def _(i):
        remote(st_send, st_recv.at[me], sends.at[1], arrivals.at[1], peer_at(me, i)).start()

    st_many = remote(
        st_recv.at[pl.ds(0, PEERS - 1)],
        st_recv.at[pl.ds(0, PEERS - 1)],
        sends.at[1],
        arrivals.at[1],
        neighbour,
    )
    st_many.wait_recv()
    st_all = st_recv[...]
    st_sum = jnp.sum(st_all, axis=0)
    live_total = limit.astype(F32) * PATCHES
    bn_mean = st_sum[0:1] / live_total
    means = st_all[:, 2:3, :] - bn_mean[None]
    shift_squares = jnp.sum(st_all[:, 3:4, :] * means * means, axis=0)
    spread = (st_sum[1:2] + shift_squares) / live_total
    gain = jnp.concatenate([gain_ref[...], gain_ref[...]], axis=1)
    bias = jnp.concatenate([bias_ref[...], bias_ref[...]], axis=1)
    bn_scale = gain * lax.rsqrt(spread + 1e-05)

    loads[3].wait()
    loads[4].wait()
    zero_half = jnp.zeros((CHANNELS, HIDDEN), BF16)
    lane_row = lax.broadcasted_iota(jnp.int32, (1, 128), 1)
    high_row = (lane_row >= CHANNELS).astype(jnp.int32) * 8

    def f_copy(c, peer):
        return remote(
            f_send.at[c, pl.ds(OWN * peer, OWN)],
            f_recv.at[:, pl.ds(pl.multiple_of(me * SENSORS + c * CHUNK, CHUNK), CHUNK), :],
            sends.at[2 + c],
            arrivals.at[2 + c],
            peer,
        )

    f_all = [
        remote(
            f_send.at[c, pl.ds(0, OWN * (PEERS - 1))],
            f_recv.at[:, pl.ds(0, CHUNK * (PEERS - 1)), :],
            sends.at[2 + c],
            arrivals.at[2 + c],
            neighbour,
        )
        for c in range(CHUNKS)
    ]
    f_self = []
    for c in range(CHUNKS):
        for gl in range(GROUPS // CHUNKS):
            g = c * (GROUPS // CHUNKS) + gl

            @pl.loop(0, 8, unroll=4)
            def _(r):
                pair = g * 8 + r
                live = (high_row + 16 * g + r < live_rows).astype(F32)
                centered = conv[g, pl.ds(r, PATCHES, stride=8), :] - bn_mean
                normed = ((centered * bn_scale + bias) * live).astype(BF16)
                normed_ref[pair] = normed
                low = dot(normed, dft[...], NT).astype(BF16)
                low_t[pair] = dot(dft[0:16, :], normed, NT).astype(BF16)
                lhs = jnp.concatenate([normed, low], axis=1)
                for half in range(2):
                    m = 16 * g + 8 * half + r
                    weight = up1[m]
                    rhs = jnp.concatenate(
                        [weight, zero_half, ufr[half]] if half == 0 else [zero_half, weight, ufr[half]],
                        axis=0,
                    )
                    value, slope = gelu_parts(dot(lhs, rhs))
                    slope_ref[m] = slope
                    feature = dot(down1[m], value.astype(BF16), NT)
                    rows32[pl.ds(16 * gl + 8 * half + r, CHANNELS, stride=CHUNK), :] = feature

        @pl.loop(0, CHANNELS, unroll=8)
        def _(d):
            at = pl.multiple_of(d * CHUNK, CHUNK)
            f_send[c, d] = rows32[pl.ds(at, CHUNK), :].astype(BF16)

        @pl.loop(1, PEERS)
        def _(i):
            f_copy(c, peer_at(me, i)).start()

        f_self.append(
            pltpu.make_async_copy(
                f_send.at[c, pl.ds(OWN * me, OWN)],
                f_recv.at[:, pl.ds(pl.multiple_of(me * SENSORS + c * CHUNK, CHUNK), CHUNK), :],
                self_sems.at[1 + c],
            )
        )
        f_self[-1].start()

    u_self.wait()
    u_all.wait_recv()

    loads[5].wait()
    loads[6].wait()
    for dd in range(OWN):
        gh_ref[dd] = dot(down2[dd], u_recv[dd]).T

    for c in range(CHUNKS):
        f_self[c].wait()
        f_all[c].wait_recv()

    for dd in range(OWN):

        def mix(b, carry):
            pre, low = carry
            at = pl.ds(pl.multiple_of(b * 256, 256), 256)
            f = f_recv[dd, at, :]
            return pre + dot(f, up2[dd, at, :], TN), low + dot(df2_ref[:, at], f)

        pre, low = lax.fori_loop(
            0,
            SLOTS // 256,
            mix,
            (jnp.zeros((PATCHES, HIDDEN), F32), jnp.zeros((8, PATCHES), F32)),
            unroll=2,
        )
        low = low.astype(BF16)
        value, slope = gelu_parts(pre + dot(low, uf2_ref[...], TN))
        hid_ref[dd] = value.astype(BF16)
        gp2 = (gh_ref[dd] * slope).astype(BF16)
        gp2_ref[dd] = gp2
        back_ref[dd] = dot(uf2_ref[...], gp2, NT).astype(BF16)
        gu2 = dot(low, gp2)
        for t in range(2):
            tile = gu2[:, 128 * t : 128 * (t + 1)]
            part[16 + t] = tile if dd == 0 else part[16 + t] + tile

    own_block = pl.ds(OWN * me, OWN)

    def g_copy(half, peer):
        return remote(
            g_send.at[half, peer],
            g_recv.at[half, own_block],
            sends.at[6 + half],
            arrivals.at[6 + half],
            peer,
        )

    def m_copy(peer):
        return remote(m_send.at[peer], m_recv.at[own_block], sends.at[8], arrivals.at[8], peer)

    g_all = [
        remote(
            g_send.at[half, pl.ds(0, PEERS - 1)],
            g_send.at[half, pl.ds(0, PEERS - 1)],
            sends.at[6 + half],
            arrivals.at[6 + half],
            neighbour,
        )
        for half in range(HALVES)
    ]
    m_all = remote(
        m_send.at[pl.ds(0, PEERS - 1)],
        m_send.at[pl.ds(0, PEERS - 1)],
        sends.at[8],
        arrivals.at[8],
        neighbour,
    )
    g_self = [
        pltpu.make_async_copy(
            g_send.at[half, me], g_recv.at[half, own_block], self_sems.at[5 + half]
        )
        for half in range(HALVES)
    ]
    m_self = pltpu.make_async_copy(m_send.at[me], m_recv.at[own_block], self_sems.at[7])

    def to_chips(copy, first):
        for i in range(4):
            for core in range(2):
                peer = 2 * chip_at(first + i) + core

                @pl.when(peer != me)
                def _():
                    copy(peer).start()

    def chip_at(i):
        return offset_peer(me, 2 * ((i + 10) % 16), 1) // 2

    @pl.loop(0, 4)
    def _(q):
        for i in range(4):
            chip = chip_at(4 * q + i)
            at = pl.ds(pl.multiple_of(chip * 128, 128), 128)
            gd2 = []
            for dd in range(OWN):
                grad = dot(up2[dd, at, :], gp2_ref[dd], NT) + dot(
                    df2_ref[:, at], back_ref[dd], TN
                )
                gd2.append(dot(back_ref[dd], f_recv[dd, at, :], NT))
                grad = grad.astype(BF16)
                for part_of in range(4):
                    core, half = part_of // 2, part_of % 2
                    g_send[half, 2 * chip + core, dd] = grad[BATCH * part_of : BATCH * (part_of + 1)]
            part[chip] = gd2[0] + gd2[1]
        to_chips(lambda peer: g_copy(0, peer), 4 * q)

    @pl.loop(0, 4)
    def _(q):
        to_chips(lambda peer: g_copy(1, peer), 4 * q)

    for half in range(HALVES):
        g_self[half].start()

    @pl.loop(0, 4)
    def _(q):
        for i in range(4):
            chip = chip_at(4 * q + i)
            at = pl.ds(pl.multiple_of(chip * 128, 128), 128)
            for dd in range(OWN):
                mix_t = dot(hid_ref[dd], down2[dd, :, at]).T.astype(BF16)
                m_send[2 * chip, dd] = mix_t[0:SENSORS]
                m_send[2 * chip + 1, dd] = mix_t[SENSORS:]
        to_chips(m_copy, 4 * q)

    m_self.start()

    gu1 = jnp.zeros((8, HIDDEN), F32)
    gd1 = jnp.zeros((16, 128), F32)
    for g in range(GROUPS):
        half_of = g // 2
        if g % 2 == 0:
            g_self[half_of].wait()
            g_all[half_of].wait_recv()

            @pl.loop(0, CHANNELS, unroll=8)
            def _(d):
                at = pl.multiple_of(d * BATCH, BATCH)
                rows32[pl.ds(at, BATCH), :] = g_recv[half_of, d].astype(F32)

        def back(r, carry):
            gu1, gd1 = carry
            pair = g * 8 + r
            grad = jnp.concatenate(
                [
                    rows32[pl.ds(16 * (g % 2) + 8 * half + r, CHANNELS, stride=BATCH), :]
                    for half in range(2)
                ],
                axis=0,
            ).T.astype(BF16)
            gps, backs = [], []
            for half in range(2):
                m = 16 * g + 8 * half + r
                weight = down1[m]
                rhs = jnp.concatenate(
                    [weight, zero_half] if half == 0 else [zero_half, weight], axis=0
                )
                gp = (dot(grad, rhs) * slope_ref[m]).astype(BF16)
                gps.append(gp)
                backs.append(dot(uf1_ref[...], gp, NT))
            low = low_t[pair].astype(F32)
            lhs = jnp.concatenate([low[0:8], low[8:16]], axis=1).astype(BF16)
            gu1 = gu1 + dot(lhs, jnp.concatenate(gps, axis=0))
            gd1 = gd1 + dot(jnp.concatenate(backs, axis=0).astype(BF16), normed_ref[pair])
            return gu1, gd1

        gu1, gd1 = lax.fori_loop(0, 8, back, (gu1, gd1), unroll=4)

    part[18] = gu1[:, 0:128]
    part[19] = gu1[:, 128:256]
    part[20] = jnp.where(lane < CHANNELS, gd1[0:8], gd1[8:16])

    part_recv[me] = part[jnp.minimum(me, TILES - 1)]

    @pl.loop(1, PEERS)
    def _(i):
        peer = peer_at(me, i)

        @pl.when(peer < TILES)
        def _():
            remote(part.at[peer], part_recv.at[me], sends.at[9], arrivals.at[9], peer).start()

    def tiles(n, ref, at):
        return remote(
            ref.at[pl.ds(0, n)], ref.at[pl.ds(0, n)], sends.at[at], arrivals.at[at], neighbour
        )

    @pl.when(me < TILES)
    def _():
        tiles(PEERS - 1, part_recv, 9).wait_recv()
        summed = jnp.sum(part_recv[...], axis=0)
        total[...] = summed
        total_recv[me] = summed

        @pl.loop(1, PEERS)
        def _(i):
            remote(
                total, total_recv.at[me], sends.at[10], arrivals.at[10], peer_at(me, i)
            ).start()

        tiles(TILES - 1, total_recv, 10).wait_recv()

    @pl.when(me >= TILES)
    def _():
        tiles(TILES, total_recv, 10).wait_recv()

    total_out[...] = total_recv[0:TILES]

    m_self.wait()
    m_all.wait_recv()
    u_all.wait_send()
    st_many.wait_send()
    for sent in f_all + g_all + [m_all]:
        sent.wait_send()

    @pl.when(me < TILES)
    def _():
        tiles(TILES - 1, part, 9).wait_send()
        tiles(PEERS - 1, total_recv, 10).wait_send()

    @pl.when(me >= TILES)
    def _():
        tiles(TILES, part, 9).wait_send()


def finish(
    count_ref, series, received, total, mixed, gd1_ref, gu1_ref, gd2_ref, gu2_ref, rows32
):
    step = pl.program_id(0)
    row = lax.broadcasted_iota(jnp.int32, (STEP, PATCHES), 0) + step * STEP
    live = (row < count_ref[0] - lax.axis_index("var") * SENSORS).astype(F32)

    @pl.loop(0, CHANNELS, unroll=16)
    def _(d):
        rows32[pl.ds(pl.multiple_of(d * STEP, STEP), STEP), :] = received[d].astype(F32) * live

    @pl.loop(0, STEP, unroll=4)
    def _(m):
        mixed[m] = (
            series[m].astype(F32) + rows32[pl.ds(m, CHANNELS, stride=STEP), :]
        ).astype(BF16)

    @pl.when(step == 0)
    def _():
        for t in range(16):
            gd2_ref[:, 128 * t : 128 * (t + 1)] = total[t]
        for t in range(2):
            gu2_ref[:, 128 * t : 128 * (t + 1)] = total[16 + t]
            gu1_ref[:, 128 * t : 128 * (t + 1)] = total[18 + t]
        both = total[20]
        gd1_ref[...] = (both + pltpu.roll(both, CHANNELS, axis=1))[:, 0:CHANNELS]


def body(
    series,
    sensor_total_count,
    depthwise_weight,
    batchnorm_gain,
    batchnorm_bias,
    channel_up_weight,
    channel_down_weight,
    down_factor1,
    up_factor1,
    sensor_up_weight,
    sensor_down_weight,
    down_factor2,
    up_factor2,
    upstream,
):
    vmem = pl.BlockSpec(memory_space=pltpu.VMEM)
    hbm = pl.BlockSpec(memory_space=pltpu.HBM)
    rows = PATCHES * 8
    dma = pltpu.SemaphoreType.DMA
    received, total = pl.pallas_call(
        kernel,
        out_shape=(
            jax.ShapeDtypeStruct((CHANNELS, SENSORS, PATCHES), BF16),
            jax.ShapeDtypeStruct((TILES, 8, 128), F32),
        ),
        in_specs=[pl.BlockSpec(memory_space=pltpu.SMEM)] + [vmem] * 6 + [hbm] * 7,
        out_specs=(hbm, vmem),
        scratch_shapes=[
            pltpu.VMEM((SENSORS, CHANNELS, PATCHES), BF16),
            pltpu.VMEM((TAPS, SENSORS, CHANNELS), BF16),
            pltpu.VMEM((SENSORS, CHANNELS, HIDDEN), BF16),
            pltpu.VMEM((SENSORS, CHANNELS, HIDDEN), BF16),
            pltpu.VMEM((OWN, SLOTS, HIDDEN), BF16),
            pltpu.VMEM((OWN, HIDDEN, SLOTS), BF16),
            pltpu.VMEM((SENSORS, CHANNELS, PATCHES), BF16),
            pltpu.VMEM((GROUPS, PADDED * 8, 128), F32),
            pltpu.VMEM((TAPS, GROUPS, 8, 128), F32),
            pltpu.VMEM((GROUPS, rows, 128), F32),
            pltpu.VMEM((SENSORS * CHANNELS, PATCHES), F32),
            pltpu.VMEM((SENSORS // 2, PATCHES, 128), BF16),
            pltpu.VMEM((SENSORS // 2, 16, PATCHES), BF16),
            pltpu.VMEM((SENSORS, PATCHES, HIDDEN), F32),
            pltpu.VMEM((CHANNELS, SENSORS, PATCHES), BF16),
            pltpu.VMEM((OWN, SLOTS, PATCHES), BF16),
            pltpu.VMEM((CHUNKS, CHANNELS, CHUNK, PATCHES), BF16),
            pltpu.VMEM((OWN, SLOTS, PATCHES), BF16),
            pltpu.VMEM((HALVES, PEERS, OWN, BATCH, PATCHES), BF16),
            pltpu.VMEM((HALVES, CHANNELS, BATCH, PATCHES), BF16),
            pltpu.VMEM((PEERS, OWN, SENSORS, PATCHES), BF16),
            pltpu.VMEM((8, 128), F32),
            pltpu.VMEM((PEERS, 8, 128), F32),
            pltpu.VMEM((128, 128), BF16),
            pltpu.VMEM((2, 128, HIDDEN), BF16),
            pltpu.VMEM((OWN, PATCHES, HIDDEN), F32),
            pltpu.VMEM((OWN, PATCHES, HIDDEN), BF16),
            pltpu.VMEM((OWN, PATCHES, HIDDEN), BF16),
            pltpu.VMEM((OWN, 8, PATCHES), BF16),
            pltpu.VMEM((PEERS, 8, 128), F32),
            pltpu.VMEM((PEERS, 8, 128), F32),
            pltpu.VMEM((8, 128), F32),
            pltpu.VMEM((PEERS, 8, 128), F32),
            dma((7,)),
            dma((8,)),
            dma((11,)),
            dma((11,)),
        ],
        compiler_params=pltpu.CompilerParams(
            collective_id=0, has_side_effects=True, vmem_limit_bytes=60 * 1024 * 1024
        ),
        cost_estimate=pl.CostEstimate(
            flops=2_000_000_000, bytes_accessed=12_000_000, transcendentals=2_200_000
        ),
    )(
        sensor_total_count,
        batchnorm_gain.reshape(1, CHANNELS),
        batchnorm_bias.reshape(1, CHANNELS),
        down_factor1.T,
        up_factor1,
        down_factor2.T,
        up_factor2,
        series[0],
        jnp.transpose(depthwise_weight, (2, 0, 1)),
        channel_up_weight,
        jnp.transpose(channel_down_weight, (0, 2, 1)),
        sensor_up_weight,
        sensor_down_weight,
        upstream[0],
    )
    whole = lambda *shape: pl.BlockSpec(shape, lambda i: (0,) * len(shape))
    sensors_block = pl.BlockSpec((STEP, CHANNELS, PATCHES), lambda i: (i, 0, 0))
    mixed, gd1, gu1, gd2, gu2 = pl.pallas_call(
        finish,
        out_shape=(
            jax.ShapeDtypeStruct((SENSORS, CHANNELS, PATCHES), BF16),
            jax.ShapeDtypeStruct((8, CHANNELS), F32),
            jax.ShapeDtypeStruct((8, HIDDEN), F32),
            jax.ShapeDtypeStruct((8, SLOTS), F32),
            jax.ShapeDtypeStruct((8, HIDDEN), F32),
        ),
        grid=(SENSORS // STEP,),
        in_specs=[
            pl.BlockSpec(memory_space=pltpu.SMEM),
            sensors_block,
            pl.BlockSpec((CHANNELS, STEP, PATCHES), lambda i: (0, i, 0)),
            whole(TILES, 8, 128),
        ],
        out_specs=(
            sensors_block,
            whole(8, CHANNELS),
            whole(8, HIDDEN),
            whole(8, SLOTS),
            whole(8, HIDDEN),
        ),
        scratch_shapes=[pltpu.VMEM((STEP * CHANNELS, PATCHES), F32)],
        compiler_params=pltpu.CompilerParams(vmem_limit_bytes=32 * 1024 * 1024),
    )(sensor_total_count, series[0], received, total)
    return mixed[None], gd1.T, gu1, gd2.T, gu2


def solution(mesh):
    placed = (
        P("grp", "var", None, None),
        P("grp"),
        P("var", None, None),
        P(),
        P(),
        P("var", None, None),
        P("var", None, None),
        P(),
        P(),
        P("var", None, None),
        P("var", None, None),
        P(),
        P(),
        P("grp", "var", None, None),
    )
    return jax.shard_map(
        body,
        mesh=mesh,
        in_specs=placed,
        out_specs=(
            P("grp", "var", None, None),
            P("grp", None),
            P("grp", None),
            P("grp", None),
            P("grp", None),
        ),
        check_vma=False,
    )
```

```python
import jax
import jax.numpy as jnp
from jax import lax
from jax.experimental import pallas as pl
from jax.experimental.pallas import tpu as pltpu
from jax.sharding import PartitionSpec as P

F32 = jnp.float32
BF16 = jnp.bfloat16
MESH = pl.DeviceIdType.MESH

tanh_scale = 0.7978845608028654
cubic_term = 0.044715

PEERS = 32
SENSORS = 64
CHANNELS = 64
PATCHES = 128
TAPS = 51
HALF = TAPS // 2
GROUPS = 4
PADDED = PATCHES + 2 * HALF
SLOTS = PEERS * SENSORS
HIDDEN = 256
OWN = 2
CHUNKS = 4
CHUNK = SENSORS // CHUNKS
HALVES = 2
BATCH = SENSORS // HALVES
TILES = 21
STEP = 16
BLOCK = 16


def gelu_parts(v):
    square = v * v
    half = 0.5 * jnp.tanh(v * (tanh_scale + (tanh_scale * cubic_term) * square)) + 0.5
    value = v * half
    slope = half + (value * (1.0 - half)) * (
        2.0 * tanh_scale + (6.0 * tanh_scale * cubic_term) * square
    )
    return value, slope


def dot(a, b, contract=((1,), (0,))):
    return lax.dot_general(a, b, (contract, ((), ())), preferred_element_type=F32)


NT = ((1,), (1,))
TN = ((0,), (0,))


def each_peer(me, act):
    for first, last, unroll in ((16, PEERS, 4), (1, 16, 5)):

        @pl.loop(first, last, unroll=unroll)
        def _(i):
            act(lax.rem(me + i, PEERS))


def kernel(
    count_ref,
    gain_ref,
    bias_ref,
    df1_ref,
    uf1_ref,
    df2_ref,
    uf2_ref,
    series_hbm,
    taps_hbm,
    up1_hbm,
    down1_hbm,
    up2_hbm,
    down2_hbm,
    upstream_hbm,
    m_recv,
    total_out,
    series,
    taps,
    up1,
    down1,
    up2,
    down2,
    upstream,
    padded,
    packed_taps,
    conv,
    rows32,
    normed_ref,
    low_t,
    slope_ref,
    u_send,
    u_recv,
    f_send,
    f_recv,
    g_send,
    g_recv,
    m_send,
    st_send,
    st_recv,
    dft,
    ufr,
    gh_ref,
    hid_ref,
    gp2_ref,
    back_ref,
    part,
    part_recv,
    total,
    total_recv,
    load_sems,
    self_sems,
    sends,
    arrivals,
):
    me = lax.axis_index("var")
    limit = count_ref[0]
    live_rows = limit - me * SENSORS

    def remote(src, dst, ssem, rsem, peer):
        return pltpu.make_async_remote_copy(
            src_ref=src,
            dst_ref=dst,
            send_sem=ssem,
            recv_sem=rsem,
            device_id={"var": peer},
            device_id_type=MESH,
        )

    loads = [
        pltpu.make_async_copy(src, dst, load_sems.at[i])
        for i, (src, dst) in enumerate(
            (
                (upstream_hbm, upstream),
                (series_hbm, series),
                (taps_hbm, taps),
                (up1_hbm, up1),
                (down1_hbm, down1),
                (down2_hbm, down2),
                (up2_hbm, up2),
            )
        )
    ]
    for load in loads:
        load.start()

    barrier = pltpu.get_barrier_semaphore()

    def greet(peer):
        pl.semaphore_signal(barrier, inc=1, device_id={"var": peer}, device_id_type=MESH)

    each_peer(me, greet)

    loads[0].wait()
    row_index = lax.broadcasted_iota(jnp.int32, (SENSORS, PATCHES), 0)
    live_sensor = (row_index < live_rows).astype(F32)

    @pl.loop(0, SENSORS, unroll=8)
    def _(m):
        rows32[pl.ds(m, CHANNELS, stride=SENSORS), :] = upstream[m].astype(F32)

    @pl.loop(0, CHANNELS, unroll=8)
    def _(d):
        at = pl.multiple_of(d * SENSORS, SENSORS)
        u_send[d] = (rows32[pl.ds(at, SENSORS), :] * live_sensor).astype(BF16)

    df1 = df1_ref[...].astype(F32)
    zero8 = jnp.zeros((8, CHANNELS), F32)
    dft[...] = jnp.concatenate(
        [
            jnp.concatenate([df1, zero8], axis=1),
            jnp.concatenate([zero8, df1], axis=1),
            jnp.zeros((112, 128), F32),
        ],
        axis=0,
    ).astype(BF16)
    uf1_32 = uf1_ref[...].astype(F32)
    ufr[0] = jnp.concatenate([uf1_32, jnp.zeros((120, HIDDEN), F32)], axis=0).astype(BF16)
    ufr[1] = jnp.concatenate(
        [jnp.zeros((8, HIDDEN), F32), uf1_32, jnp.zeros((112, HIDDEN), F32)], axis=0
    ).astype(BF16)

    loads[1].wait()
    loads[2].wait()
    padded[:, 0 : HALF * 8, :] = jnp.zeros((GROUPS, HALF * 8, 128), F32)
    padded[:, (HALF + PATCHES) * 8 : PADDED * 8, :] = jnp.zeros((GROUPS, HALF * 8, 128), F32)

    for g in range(GROUPS):

        @pl.loop(0, 8, unroll=8)
        def _(r):
            both = jnp.concatenate(
                [series[16 * g + r].astype(F32), series[16 * g + 8 + r].astype(F32)], axis=0
            )
            padded[g, pl.ds(HALF * 8 + r, PATCHES, stride=8), :] = both.T

    @pl.loop(0, TAPS, unroll=3)
    def _(k):
        row = taps[k].astype(F32)
        for g in range(GROUPS):
            packed_taps[k, g] = jnp.concatenate(
                [row[16 * g : 16 * g + 8], row[16 * g + 8 : 16 * g + 16]], axis=1
            )

    pl.semaphore_wait(barrier, PEERS - 1)
    mine = pl.ds(pl.multiple_of(me * SENSORS, SENSORS), SENSORS)
    neighbour = lax.rem(me + 1, PEERS)

    def u_start(peer):
        remote(
            u_send.at[pl.ds(OWN * peer, OWN)], u_recv.at[:, mine, :], sends.at[0], arrivals.at[0], peer
        ).start()

    each_peer(me, u_start)
    u_self = pltpu.make_async_copy(
        u_send.at[pl.ds(OWN * me, OWN)], u_recv.at[:, mine, :], self_sems.at[0]
    )
    u_self.start()
    u_all = remote(
        u_send.at[pl.ds(0, OWN * (PEERS - 1))],
        u_recv.at[:, pl.ds(0, SENSORS * (PEERS - 1)), :],
        sends.at[0],
        arrivals.at[0],
        neighbour,
    )

    sub = lax.broadcasted_iota(jnp.int32, (8, 128), 0)
    lane = lax.broadcasted_iota(jnp.int32, (8, 128), 1)
    high = (lane >= CHANNELS).astype(jnp.int32) * 8

    def group_mask(g):
        return (sub + high + 16 * g < live_rows).astype(F32)

    def conv_group(g, sums):
        def conv_block(nb, acc_sum):
            base = pl.multiple_of(nb * (BLOCK * 8), BLOCK * 8)
            acc = [None] * BLOCK
            tap = {}
            for j in range(BLOCK + TAPS - 1):
                x = padded[g, pl.ds(base + 8 * j, 8), :]
                if j < TAPS:
                    tap[j] = packed_taps[j, g]
                for i in range(max(0, j - TAPS + 1), min(BLOCK - 1, j) + 1):
                    term = tap[j - i] * x
                    acc[i] = term if acc[i] is None else acc[i] + term
            for i in range(BLOCK):
                conv[g, pl.ds(base + 8 * i, 8), :] = acc[i]
                acc_sum = acc_sum + acc[i]
            return acc_sum

        group_sum = lax.fori_loop(0, PATCHES // BLOCK, conv_block, jnp.zeros((8, 128), F32))
        return sums + group_sum * group_mask(g)

    sums = lax.fori_loop(0, GROUPS, conv_group, jnp.zeros((8, 128), F32))

    def fold(v):
        v = jnp.sum(v, axis=0, keepdims=True)
        return v + pltpu.roll(v, CHANNELS, axis=1)

    sum_row = fold(sums)
    own_count = jnp.clip(live_rows, 0, SENSORS).astype(F32) * PATCHES
    own_mean = sum_row / jnp.maximum(own_count, 1.0)

    def square_group(g, squares):
        def block(b, acc):
            at = pl.multiple_of(b * 128, 128)
            c = conv[g, pl.ds(at, 128), :] - own_mean
            return acc + jnp.sum((c * c).reshape(16, 8, 128), axis=0)

        group = lax.fori_loop(0, 8, block, jnp.zeros((8, 128), F32))
        return squares + group * group_mask(g)

    square_row = fold(lax.fori_loop(0, GROUPS, square_group, jnp.zeros((8, 128), F32)))
    stats = jnp.where(
        sub == 0,
        sum_row,
        jnp.where(sub == 1, square_row, jnp.where(sub == 2, own_mean, own_count)),
    )
    st_send[...] = stats
    st_recv[me] = stats

    each_peer(
        me,
        lambda peer: remote(
            st_send, st_recv.at[me], sends.at[1], arrivals.at[1], peer
        ).start(),
    )

    st_many = remote(
        st_recv.at[pl.ds(0, PEERS - 1)],
        st_recv.at[pl.ds(0, PEERS - 1)],
        sends.at[1],
        arrivals.at[1],
        neighbour,
    )
    st_many.wait_recv()
    st_all = st_recv[...]
    st_sum = jnp.sum(st_all, axis=0)
    live_total = limit.astype(F32) * PATCHES
    bn_mean = st_sum[0:1] / live_total
    means = st_all[:, 2:3, :] - bn_mean[None]
    shift_squares = jnp.sum(st_all[:, 3:4, :] * means * means, axis=0)
    spread = (st_sum[1:2] + shift_squares) / live_total
    gain = jnp.concatenate([gain_ref[...], gain_ref[...]], axis=1)
    bias = jnp.concatenate([bias_ref[...], bias_ref[...]], axis=1)
    bn_scale = gain * lax.rsqrt(spread + 1e-05)

    loads[3].wait()
    loads[4].wait()
    zero_half = jnp.zeros((CHANNELS, HIDDEN), BF16)
    lane_row = lax.broadcasted_iota(jnp.int32, (1, 128), 1)
    high_row = (lane_row >= CHANNELS).astype(jnp.int32) * 8

    def f_copy(c, peer):
        return remote(
            f_send.at[c, pl.ds(OWN * peer, OWN)],
            f_recv.at[:, pl.ds(pl.multiple_of(me * SENSORS + c * CHUNK, CHUNK), CHUNK), :],
            sends.at[2 + c],
            arrivals.at[2 + c],
            peer,
        )

    f_all = [
        remote(
            f_send.at[c, pl.ds(0, OWN * (PEERS - 1))],
            f_recv.at[:, pl.ds(0, CHUNK * (PEERS - 1)), :],
            sends.at[2 + c],
            arrivals.at[2 + c],
            neighbour,
        )
        for c in range(CHUNKS)
    ]
    f_self = []
    for c in range(CHUNKS):
        for gl in range(GROUPS // CHUNKS):
            g = c * (GROUPS // CHUNKS) + gl

            @pl.loop(0, 8, unroll=8)
            def _(r):
                pair = g * 8 + r
                live = (high_row + 16 * g + r < live_rows).astype(F32)
                centered = conv[g, pl.ds(r, PATCHES, stride=8), :] - bn_mean
                normed = ((centered * bn_scale + bias) * live).astype(BF16)
                normed_ref[pair] = normed
                low = dot(normed, dft[...], NT).astype(BF16)
                low_t[pair] = dot(dft[0:16, :], normed, NT).astype(BF16)
                lhs = jnp.concatenate([normed, low], axis=1)
                for half in range(2):
                    m = 16 * g + 8 * half + r
                    weight = up1[m]
                    rhs = jnp.concatenate(
                        [weight, zero_half, ufr[half]] if half == 0 else [zero_half, weight, ufr[half]],
                        axis=0,
                    )
                    value, slope = gelu_parts(dot(lhs, rhs))
                    slope_ref[m] = slope
                    feature = dot(down1[m], value.astype(BF16), NT)
                    rows32[pl.ds(16 * gl + 8 * half + r, CHANNELS, stride=CHUNK), :] = feature

        @pl.loop(0, CHANNELS, unroll=8)
        def _(d):
            at = pl.multiple_of(d * CHUNK, CHUNK)
            f_send[c, d] = rows32[pl.ds(at, CHUNK), :].astype(BF16)

        each_peer(me, lambda peer: f_copy(c, peer).start())

        f_self.append(
            pltpu.make_async_copy(
                f_send.at[c, pl.ds(OWN * me, OWN)],
                f_recv.at[:, pl.ds(pl.multiple_of(me * SENSORS + c * CHUNK, CHUNK), CHUNK), :],
                self_sems.at[1 + c],
            )
        )
        f_self[-1].start()

    u_self.wait()
    u_all.wait_recv()

    loads[5].wait()
    loads[6].wait()
    for dd in range(OWN):
        gh_ref[dd] = dot(down2[dd], u_recv[dd]).T

    for c in range(CHUNKS):
        f_self[c].wait()
        f_all[c].wait_recv()

    for dd in range(OWN):

        def mix(b, carry):
            pre, low = carry
            at = pl.ds(pl.multiple_of(b * 256, 256), 256)
            f = f_recv[dd, at, :]
            return pre + dot(f, up2[dd, at, :], TN), low + dot(df2_ref[:, at], f)

        pre, low = lax.fori_loop(
            0,
            SLOTS // 256,
            mix,
            (jnp.zeros((PATCHES, HIDDEN), F32), jnp.zeros((8, PATCHES), F32)),
            unroll=2,
        )
        low = low.astype(BF16)
        value, slope = gelu_parts(pre + dot(low, uf2_ref[...], TN))
        hid_ref[dd] = value.astype(BF16)
        gp2 = (gh_ref[dd] * slope).astype(BF16)
        gp2_ref[dd] = gp2
        back_ref[dd] = dot(uf2_ref[...], gp2, NT).astype(BF16)
        gu2 = dot(low, gp2)
        for t in range(2):
            tile = gu2[:, 128 * t : 128 * (t + 1)]
            part[16 + t] = tile if dd == 0 else part[16 + t] + tile

    own_block = pl.ds(OWN * me, OWN)

    def g_copy(half, peer):
        return remote(
            g_send.at[half, peer],
            g_recv.at[half, own_block],
            sends.at[6 + half],
            arrivals.at[6 + half],
            peer,
        )

    def m_copy(peer):
        return remote(m_send.at[peer], m_recv.at[own_block], sends.at[8], arrivals.at[8], peer)

    g_all = [
        remote(
            g_send.at[half, pl.ds(0, PEERS - 1)],
            g_send.at[half, pl.ds(0, PEERS - 1)],
            sends.at[6 + half],
            arrivals.at[6 + half],
            neighbour,
        )
        for half in range(HALVES)
    ]
    m_all = remote(
        m_send.at[pl.ds(0, PEERS - 1)],
        m_send.at[pl.ds(0, PEERS - 1)],
        sends.at[8],
        arrivals.at[8],
        neighbour,
    )
    g_self = [
        pltpu.make_async_copy(
            g_send.at[half, me], g_recv.at[half, own_block], self_sems.at[5 + half]
        )
        for half in range(HALVES)
    ]
    m_self = pltpu.make_async_copy(m_send.at[me], m_recv.at[own_block], self_sems.at[7])

    own_chip = me // 2
    sibling = 2 * own_chip + 1 - lax.rem(me, 2)

    def chip_at(i):
        return lax.rem(own_chip + 1 + lax.rem(i + 7, 15), 16)

    def each_chip(act, send):
        @pl.loop(0, 5)
        def _(q):
            chips = [chip_at(3 * q + i) for i in range(3)]
            if act is not None:
                for chip in chips:
                    act(chip)
            for chip in chips:
                send(2 * chip)
                send(2 * chip + 1)

        if act is not None:
            act(own_chip)
        send(sibling)

    def g_block(chip):
        at = pl.ds(pl.multiple_of(chip * 128, 128), 128)
        gd2 = []
        for dd in range(OWN):
            grad = dot(up2[dd, at, :], gp2_ref[dd], NT) + dot(df2_ref[:, at], back_ref[dd], TN)
            gd2.append(dot(back_ref[dd], f_recv[dd, at, :], NT))
            grad = grad.astype(BF16)
            for part_of in range(4):
                core, half = part_of // 2, part_of % 2
                g_send[half, 2 * chip + core, dd] = grad[BATCH * part_of : BATCH * (part_of + 1)]
        part[chip] = gd2[0] + gd2[1]

    def m_block(chip):
        at = pl.ds(pl.multiple_of(chip * 128, 128), 128)
        for dd in range(OWN):
            mix_t = dot(hid_ref[dd], down2[dd, :, at]).T.astype(BF16)
            m_send[2 * chip, dd] = mix_t[0:SENSORS]
            m_send[2 * chip + 1, dd] = mix_t[SENSORS:]

    each_chip(g_block, lambda peer: g_copy(0, peer).start())
    each_chip(None, lambda peer: g_copy(1, peer).start())
    for half in range(HALVES):
        g_self[half].start()

    def tiles(n, ref, at):
        return remote(
            ref.at[pl.ds(0, n)], ref.at[pl.ds(0, n)], sends.at[at], arrivals.at[at], neighbour
        )

    def is_owner(device, first, last):
        return jnp.logical_and(device >= first, device < last)

    def to_owners(first, last, at):
        @pl.loop(first, last)
        def _(owner):
            @pl.when(owner != me)
            def _():
                remote(
                    part.at[owner], part_recv.at[me], sends.at[at], arrivals.at[at], owner
                ).start()

        @pl.when(is_owner(me, first, last))
        def _():
            part_recv[me] = part[me]

    def from_owners(first, last, at):
        @pl.when(is_owner(me, first, last))
        def _():
            tiles(PEERS - 1, part_recv, at).wait_recv()
            summed = jnp.sum(part_recv[...], axis=0)
            total[...] = summed
            total_recv[me] = summed
            each_peer(
                me,
                lambda peer: remote(
                    total, total_recv.at[me], sends.at[at + 1], arrivals.at[at + 1], peer
                ).start(),
            )

    def by_role(first, last, owner_act, other_act):
        owner = is_owner(me, first, last)
        pl.when(owner)(owner_act)
        pl.when(jnp.logical_not(owner))(other_act)

    def totals_arrive(first, last, at):
        by_role(
            first,
            last,
            lambda: tiles(last - first - 1, total_recv, at + 1).wait_recv(),
            lambda: tiles(last - first, total_recv, at + 1).wait_recv(),
        )

    def totals_left(first, last, at):
        def owner_act():
            tiles(last - first - 1, part, at).wait_send()
            tiles(PEERS - 1, total_recv, at + 1).wait_send()

        by_role(first, last, owner_act, lambda: tiles(last - first, part, at).wait_send())

    to_owners(0, 18, 9)

    each_chip(m_block, lambda peer: m_copy(peer).start())
    m_self.start()

    gu1 = jnp.zeros((8, HIDDEN), F32)
    gd1 = jnp.zeros((16, 128), F32)
    for g in range(GROUPS):
        half_of = g // 2
        if g == 2:
            from_owners(0, 18, 9)
        if g % 2 == 0:
            g_self[half_of].wait()
            g_all[half_of].wait_recv()

            @pl.loop(0, CHANNELS, unroll=8)
            def _(d):
                at = pl.multiple_of(d * BATCH, BATCH)
                rows32[pl.ds(at, BATCH), :] = g_recv[half_of, d].astype(F32)

        def back(r, carry):
            gu1, gd1 = carry
            pair = g * 8 + r
            grad = jnp.concatenate(
                [
                    rows32[pl.ds(16 * (g % 2) + 8 * half + r, CHANNELS, stride=BATCH), :]
                    for half in range(2)
                ],
                axis=0,
            ).T.astype(BF16)
            gps, backs = [], []
            for half in range(2):
                m = 16 * g + 8 * half + r
                weight = down1[m]
                rhs = jnp.concatenate(
                    [weight, zero_half] if half == 0 else [zero_half, weight], axis=0
                )
                gp = (dot(grad, rhs) * slope_ref[m]).astype(BF16)
                gps.append(gp)
                backs.append(dot(uf1_ref[...], gp, NT))
            low = low_t[pair].astype(F32)
            lhs = jnp.concatenate([low[0:8], low[8:16]], axis=1).astype(BF16)
            gu1 = gu1 + dot(lhs, jnp.concatenate(gps, axis=0))
            gd1 = gd1 + dot(jnp.concatenate(backs, axis=0).astype(BF16), normed_ref[pair])
            return gu1, gd1

        gu1, gd1 = lax.fori_loop(0, 8, back, (gu1, gd1), unroll=8)

    part[18] = gu1[:, 0:128]
    part[19] = gu1[:, 128:256]
    part[20] = jnp.where(lane < CHANNELS, gd1[0:8], gd1[8:16])

    to_owners(18, TILES, 11)
    from_owners(18, TILES, 11)
    totals_arrive(0, 18, 9)
    totals_arrive(18, TILES, 11)
    total_out[...] = total_recv[0:TILES]

    m_self.wait()
    m_all.wait_recv()
    u_all.wait_send()
    st_many.wait_send()
    for sent in f_all + g_all + [m_all]:
        sent.wait_send()

    totals_left(0, 18, 9)
    totals_left(18, TILES, 11)


def finish(
    count_ref,
    series_hbm,
    received_hbm,
    total_hbm,
    mixed_hbm,
    gd1_ref,
    gu1_ref,
    gd2_ref,
    gu2_ref,
    series,
    received,
    total,
    mixed,
    rows32,
    load_sems,
    store_sems,
):
    steps = SENSORS // STEP
    loads = [
        pltpu.make_async_copy(
            received_hbm.at[:, pl.ds(step * STEP, STEP), :], received.at[step], load_sems.at[step]
        )
        for step in range(steps)
    ]
    loads.append(pltpu.make_async_copy(total_hbm, total, load_sems.at[steps]))
    blocks = [pl.ds(step * STEP, STEP) for step in range(steps)]
    series_loads = [
        pltpu.make_async_copy(
            series_hbm.at[blocks[step]], series.at[blocks[step]], load_sems.at[steps + 1 + step]
        )
        for step in range(steps)
    ]
    for step in range(steps):
        loads[step].start()
        series_loads[step].start()
    loads[steps].start()
    live_rows = count_ref[0] - lax.axis_index("var") * SENSORS
    row = lax.broadcasted_iota(jnp.int32, (STEP, PATCHES), 0)
    stores = []
    for step in range(steps):
        loads[step].wait()
        series_loads[step].wait()
        live = (row + step * STEP < live_rows).astype(F32)

        @pl.loop(0, CHANNELS, unroll=16)
        def _(d):
            rows32[pl.ds(pl.multiple_of(d * STEP, STEP), STEP), :] = (
                received[step, d].astype(F32) * live
            )

        @pl.loop(0, STEP, unroll=8)
        def _(m):
            mixed[step * STEP + m] = (
                series[step * STEP + m].astype(F32) + rows32[pl.ds(m, CHANNELS, stride=STEP), :]
            ).astype(BF16)

        stores.append(
            pltpu.make_async_copy(
                mixed.at[blocks[step]], mixed_hbm.at[blocks[step]], store_sems.at[step]
            )
        )
        stores[-1].start()

    loads[steps].wait()
    for t in range(16):
        gd2_ref[:, 128 * t : 128 * (t + 1)] = total[t]
    for t in range(2):
        gu2_ref[:, 128 * t : 128 * (t + 1)] = total[16 + t]
        gu1_ref[:, 128 * t : 128 * (t + 1)] = total[18 + t]
    both = total[20]
    gd1_ref[...] = (both + pltpu.roll(both, CHANNELS, axis=1))[:, 0:CHANNELS]
    for store in stores:
        store.wait()


def body(
    series,
    sensor_total_count,
    depthwise_weight,
    batchnorm_gain,
    batchnorm_bias,
    channel_up_weight,
    channel_down_weight,
    down_factor1,
    up_factor1,
    sensor_up_weight,
    sensor_down_weight,
    down_factor2,
    up_factor2,
    upstream,
):
    vmem = pl.BlockSpec(memory_space=pltpu.VMEM)
    hbm = pl.BlockSpec(memory_space=pltpu.HBM)
    rows = PATCHES * 8
    dma = pltpu.SemaphoreType.DMA
    received, total = pl.pallas_call(
        kernel,
        out_shape=(
            jax.ShapeDtypeStruct((CHANNELS, SENSORS, PATCHES), BF16),
            jax.ShapeDtypeStruct((TILES, 8, 128), F32),
        ),
        in_specs=[pl.BlockSpec(memory_space=pltpu.SMEM)] + [vmem] * 6 + [hbm] * 7,
        out_specs=(hbm, vmem),
        scratch_shapes=[
            pltpu.VMEM((SENSORS, CHANNELS, PATCHES), BF16),
            pltpu.VMEM((TAPS, SENSORS, CHANNELS), BF16),
            pltpu.VMEM((SENSORS, CHANNELS, HIDDEN), BF16),
            pltpu.VMEM((SENSORS, CHANNELS, HIDDEN), BF16),
            pltpu.VMEM((OWN, SLOTS, HIDDEN), BF16),
            pltpu.VMEM((OWN, HIDDEN, SLOTS), BF16),
            pltpu.VMEM((SENSORS, CHANNELS, PATCHES), BF16),
            pltpu.VMEM((GROUPS, PADDED * 8, 128), F32),
            pltpu.VMEM((TAPS, GROUPS, 8, 128), F32),
            pltpu.VMEM((GROUPS, rows, 128), F32),
            pltpu.VMEM((SENSORS * CHANNELS, PATCHES), F32),
            pltpu.VMEM((SENSORS // 2, PATCHES, 128), BF16),
            pltpu.VMEM((SENSORS // 2, 16, PATCHES), BF16),
            pltpu.VMEM((SENSORS, PATCHES, HIDDEN), F32),
            pltpu.VMEM((CHANNELS, SENSORS, PATCHES), BF16),
            pltpu.VMEM((OWN, SLOTS, PATCHES), BF16),
            pltpu.VMEM((CHUNKS, CHANNELS, CHUNK, PATCHES), BF16),
            pltpu.VMEM((OWN, SLOTS, PATCHES), BF16),
            pltpu.VMEM((HALVES, PEERS, OWN, BATCH, PATCHES), BF16),
            pltpu.VMEM((HALVES, CHANNELS, BATCH, PATCHES), BF16),
            pltpu.VMEM((PEERS, OWN, SENSORS, PATCHES), BF16),
            pltpu.VMEM((8, 128), F32),
            pltpu.VMEM((PEERS, 8, 128), F32),
            pltpu.VMEM((128, 128), BF16),
            pltpu.VMEM((2, 128, HIDDEN), BF16),
            pltpu.VMEM((OWN, PATCHES, HIDDEN), F32),
            pltpu.VMEM((OWN, PATCHES, HIDDEN), BF16),
            pltpu.VMEM((OWN, PATCHES, HIDDEN), BF16),
            pltpu.VMEM((OWN, 8, PATCHES), BF16),
            pltpu.VMEM((PEERS, 8, 128), F32),
            pltpu.VMEM((PEERS, 8, 128), F32),
            pltpu.VMEM((8, 128), F32),
            pltpu.VMEM((PEERS, 8, 128), F32),
            dma((7,)),
            dma((8,)),
            dma((13,)),
            dma((13,)),
        ],
        compiler_params=pltpu.CompilerParams(
            collective_id=0, has_side_effects=True, vmem_limit_bytes=60 * 1024 * 1024
        ),
        cost_estimate=pl.CostEstimate(
            flops=2_000_000_000, bytes_accessed=12_000_000, transcendentals=2_200_000
        ),
    )(
        sensor_total_count,
        batchnorm_gain.reshape(1, CHANNELS),
        batchnorm_bias.reshape(1, CHANNELS),
        down_factor1.T,
        up_factor1,
        down_factor2.T,
        up_factor2,
        series[0],
        jnp.transpose(depthwise_weight, (2, 0, 1)),
        channel_up_weight,
        jnp.transpose(channel_down_weight, (0, 2, 1)),
        sensor_up_weight,
        sensor_down_weight,
        upstream[0],
    )
    mixed, gd1, gu1, gd2, gu2 = pl.pallas_call(
        finish,
        out_shape=(
            jax.ShapeDtypeStruct((SENSORS, CHANNELS, PATCHES), BF16),
            jax.ShapeDtypeStruct((8, CHANNELS), F32),
            jax.ShapeDtypeStruct((8, HIDDEN), F32),
            jax.ShapeDtypeStruct((8, SLOTS), F32),
            jax.ShapeDtypeStruct((8, HIDDEN), F32),
        ),
        in_specs=[pl.BlockSpec(memory_space=pltpu.SMEM), hbm, hbm, hbm],
        out_specs=(hbm, vmem, vmem, vmem, vmem),
        scratch_shapes=[
            pltpu.VMEM((SENSORS, CHANNELS, PATCHES), BF16),
            pltpu.VMEM((SENSORS // STEP, CHANNELS, STEP, PATCHES), BF16),
            pltpu.VMEM((TILES, 8, 128), F32),
            pltpu.VMEM((SENSORS, CHANNELS, PATCHES), BF16),
            pltpu.VMEM((STEP * CHANNELS, PATCHES), F32),
            dma((2 * (SENSORS // STEP) + 1,)),
            dma((SENSORS // STEP,)),
        ],
        compiler_params=pltpu.CompilerParams(vmem_limit_bytes=60 * 1024 * 1024),
    )(sensor_total_count, series[0], received, total)
    return mixed[None], gd1.T, gu1, gd2.T, gu2


def solution(mesh):
    placed = (
        P("grp", "var", None, None),
        P("grp"),
        P("var", None, None),
        P(),
        P(),
        P("var", None, None),
        P("var", None, None),
        P(),
        P(),
        P("var", None, None),
        P("var", None, None),
        P(),
        P(),
        P("grp", "var", None, None),
    )
    return jax.shard_map(
        body,
        mesh=mesh,
        in_specs=placed,
        out_specs=(
            P("grp", "var", None, None),
            P("grp", None),
            P("grp", None),
            P("grp", None),
            P("grp", None),
        ),
        check_vma=False,
    )
```

```python
import jax
import jax.numpy as jnp
from jax import lax
from jax.experimental import pallas as pl
from jax.experimental.pallas import tpu as pltpu
from jax.sharding import PartitionSpec as P

F32 = jnp.float32
BF16 = jnp.bfloat16
MESH = pl.DeviceIdType.MESH

tanh_scale = 0.7978845608028654
cubic_term = 0.044715

PEERS = 32
SENSORS = 64
CHANNELS = 64
PATCHES = 128
TAPS = 51
HALF = TAPS // 2
GROUPS = 4
PADDED = PATCHES + 2 * HALF
SLOTS = PEERS * SENSORS
HIDDEN = 256
OWN = 2
CHUNKS = 4
CHUNK = SENSORS // CHUNKS
HALVES = 2
BATCH = SENSORS // HALVES
TILES = 21
FIRST_SENDS = 7
ORDER = tuple(range(16, PEERS)) + tuple(range(1, 16))
STEP = 16
BLOCK = 16


def gelu_parts(v):
    square = v * v
    half = 0.5 * jnp.tanh(v * (tanh_scale + (tanh_scale * cubic_term) * square)) + 0.5
    value = v * half
    slope = half + (value * (1.0 - half)) * (
        2.0 * tanh_scale + (6.0 * tanh_scale * cubic_term) * square
    )
    return value, slope


def dot(a, b, contract=((1,), (0,))):
    return lax.dot_general(a, b, (contract, ((), ())), preferred_element_type=F32)


NT = ((1,), (1,))
TN = ((0,), (0,))


def each_peer(me, act):
    for first, last, unroll in ((16, PEERS, 4), (1, 16, 5)):

        @pl.loop(first, last, unroll=unroll)
        def _(i):
            act(lax.rem(me + i, PEERS))


def kernel(
    count_ref,
    gain_ref,
    bias_ref,
    df1_ref,
    uf1_ref,
    df2_ref,
    uf2_ref,
    series_hbm,
    taps_hbm,
    up1_hbm,
    down1_hbm,
    up2_hbm,
    down2_hbm,
    upstream_hbm,
    m_recv,
    total_out,
    series,
    taps,
    up1,
    down1,
    up2,
    down2,
    upstream,
    padded,
    packed_taps,
    conv,
    rows32,
    normed_ref,
    low_t,
    slope_ref,
    u_send,
    u_recv,
    f_send,
    f_recv,
    g_send,
    g_recv,
    m_send,
    st_send,
    st_recv,
    dft,
    ufr,
    gh_ref,
    hid_ref,
    gp2_ref,
    back_ref,
    part,
    part_recv,
    total,
    total_recv,
    load_sems,
    self_sems,
    sends,
    arrivals,
):
    me = lax.axis_index("var")
    limit = count_ref[0]
    live_rows = limit - me * SENSORS

    def remote(src, dst, ssem, rsem, peer):
        return pltpu.make_async_remote_copy(
            src_ref=src,
            dst_ref=dst,
            send_sem=ssem,
            recv_sem=rsem,
            device_id={"var": peer},
            device_id_type=MESH,
        )

    loads = [
        pltpu.make_async_copy(src, dst, load_sems.at[i])
        for i, (src, dst) in enumerate(
            (
                (upstream_hbm, upstream),
                (series_hbm, series),
                (taps_hbm, taps),
                (up1_hbm, up1),
                (down1_hbm, down1),
                (down2_hbm, down2),
                (up2_hbm, up2),
            )
        )
    ]
    for load in loads[:3]:
        load.start()

    barrier = pltpu.get_barrier_semaphore()

    def greet(peer):
        pl.semaphore_signal(barrier, inc=1, device_id={"var": peer}, device_id_type=MESH)

    each_peer(me, greet)

    loads[0].wait()
    row_index = lax.broadcasted_iota(jnp.int32, (SENSORS, PATCHES), 0)
    live_sensor = (row_index < live_rows).astype(F32)

    @pl.loop(0, SENSORS, unroll=8)
    def _(m):
        rows32[pl.ds(m, CHANNELS, stride=SENSORS), :] = upstream[m].astype(F32)

    @pl.loop(0, CHANNELS, unroll=8)
    def _(d):
        at = pl.multiple_of(d * SENSORS, SENSORS)
        u_send[d] = (rows32[pl.ds(at, SENSORS), :] * live_sensor).astype(BF16)

    df1 = df1_ref[...].astype(F32)
    zero8 = jnp.zeros((8, CHANNELS), F32)
    dft[...] = jnp.concatenate(
        [
            jnp.concatenate([df1, zero8], axis=1),
            jnp.concatenate([zero8, df1], axis=1),
            jnp.zeros((112, 128), F32),
        ],
        axis=0,
    ).astype(BF16)
    uf1_32 = uf1_ref[...].astype(F32)
    ufr[0] = jnp.concatenate([uf1_32, jnp.zeros((120, HIDDEN), F32)], axis=0).astype(BF16)
    ufr[1] = jnp.concatenate(
        [jnp.zeros((8, HIDDEN), F32), uf1_32, jnp.zeros((112, HIDDEN), F32)], axis=0
    ).astype(BF16)

    loads[1].wait()
    loads[2].wait()
    for load in loads[3:]:
        load.start()
    padded[:, 0 : HALF * 8, :] = jnp.zeros((GROUPS, HALF * 8, 128), F32)
    padded[:, (HALF + PATCHES) * 8 : PADDED * 8, :] = jnp.zeros((GROUPS, HALF * 8, 128), F32)

    for g in range(GROUPS):

        @pl.loop(0, 8, unroll=8)
        def _(r):
            both = jnp.concatenate(
                [series[16 * g + r].astype(F32), series[16 * g + 8 + r].astype(F32)], axis=0
            )
            padded[g, pl.ds(HALF * 8 + r, PATCHES, stride=8), :] = both.T

    @pl.loop(0, TAPS, unroll=3)
    def _(k):
        row = taps[k].astype(F32)
        for g in range(GROUPS):
            packed_taps[k, g] = jnp.concatenate(
                [row[16 * g : 16 * g + 8], row[16 * g + 8 : 16 * g + 16]], axis=1
            )

    pl.semaphore_wait(barrier, PEERS - 1)
    mine = pl.ds(pl.multiple_of(me * SENSORS, SENSORS), SENSORS)
    neighbour = lax.rem(me + 1, PEERS)

    def u_start(peer):
        remote(
            u_send.at[pl.ds(OWN * peer, OWN)], u_recv.at[:, mine, :], sends.at[0], arrivals.at[0], peer
        ).start()

    for offset in range(FIRST_SENDS):
        u_start(lax.rem(me + PEERS - 1 - offset, PEERS))
    u_self = pltpu.make_async_copy(
        u_send.at[pl.ds(OWN * me, OWN)], u_recv.at[:, mine, :], self_sems.at[0]
    )
    u_self.start()
    u_all = remote(
        u_send.at[pl.ds(0, OWN * (PEERS - 1))],
        u_recv.at[:, pl.ds(0, SENSORS * (PEERS - 1)), :],
        sends.at[0],
        arrivals.at[0],
        neighbour,
    )

    sub = lax.broadcasted_iota(jnp.int32, (8, 128), 0)
    lane = lax.broadcasted_iota(jnp.int32, (8, 128), 1)
    high = (lane >= CHANNELS).astype(jnp.int32) * 8

    def group_mask(g):
        return (sub + high + 16 * g < live_rows).astype(F32)

    def conv_group(g, sums, sending=True):
        def conv_block(nb, acc_sum):
            if sending:
                u_start(lax.rem(me + 1 + 8 * g + nb, PEERS))
            base = pl.multiple_of(nb * (BLOCK * 8), BLOCK * 8)
            acc = [None] * BLOCK
            tap = {}
            for j in range(BLOCK + TAPS - 1):
                x = padded[g, pl.ds(base + 8 * j, 8), :]
                if j < TAPS:
                    tap[j] = packed_taps[j, g]
                for i in range(max(0, j - TAPS + 1), min(BLOCK - 1, j) + 1):
                    term = tap[j - i] * x
                    acc[i] = term if acc[i] is None else acc[i] + term
            for i in range(BLOCK):
                conv[g, pl.ds(base + 8 * i, 8), :] = acc[i]
                acc_sum = acc_sum + acc[i]
            return acc_sum

        group_sum = lax.fori_loop(0, PATCHES // BLOCK, conv_block, jnp.zeros((8, 128), F32))
        return sums + group_sum * group_mask(g)

    sums = lax.fori_loop(0, GROUPS - 1, conv_group, jnp.zeros((8, 128), F32))
    sums = conv_group(GROUPS - 1, sums, sending=False)

    def fold(v):
        v = jnp.sum(v, axis=0, keepdims=True)
        return v + pltpu.roll(v, CHANNELS, axis=1)

    sum_row = fold(sums)
    own_count = jnp.clip(live_rows, 0, SENSORS).astype(F32) * PATCHES
    own_mean = sum_row / jnp.maximum(own_count, 1.0)

    def square_group(g, squares):
        def block(b, acc):
            at = pl.multiple_of(b * 128, 128)
            c = conv[g, pl.ds(at, 128), :] - own_mean
            return acc + jnp.sum((c * c).reshape(16, 8, 128), axis=0)

        group = lax.fori_loop(0, 8, block, jnp.zeros((8, 128), F32))
        return squares + group * group_mask(g)

    square_row = fold(lax.fori_loop(0, GROUPS, square_group, jnp.zeros((8, 128), F32)))
    stats = jnp.where(
        sub == 0,
        sum_row,
        jnp.where(sub == 1, square_row, jnp.where(sub == 2, own_mean, own_count)),
    )
    st_send[...] = stats
    st_recv[me] = stats

    each_peer(
        me,
        lambda peer: remote(
            st_send, st_recv.at[me], sends.at[1], arrivals.at[1], peer
        ).start(),
    )

    st_many = remote(
        st_recv.at[pl.ds(0, PEERS - 1)],
        st_recv.at[pl.ds(0, PEERS - 1)],
        sends.at[1],
        arrivals.at[1],
        neighbour,
    )
    st_many.wait_recv()
    st_all = st_recv[...]
    st_sum = jnp.sum(st_all, axis=0)
    live_total = limit.astype(F32) * PATCHES
    bn_mean = st_sum[0:1] / live_total
    means = st_all[:, 2:3, :] - bn_mean[None]
    shift_squares = jnp.sum(st_all[:, 3:4, :] * means * means, axis=0)
    spread = (st_sum[1:2] + shift_squares) / live_total
    gain = jnp.concatenate([gain_ref[...], gain_ref[...]], axis=1)
    bias = jnp.concatenate([bias_ref[...], bias_ref[...]], axis=1)
    bn_scale = gain * lax.rsqrt(spread + 1e-05)

    loads[3].wait()
    loads[4].wait()
    zero_half = jnp.zeros((CHANNELS, HIDDEN), BF16)
    lane_row = lax.broadcasted_iota(jnp.int32, (1, 128), 1)
    high_row = (lane_row >= CHANNELS).astype(jnp.int32) * 8

    def f_copy(c, peer):
        return remote(
            f_send.at[c, pl.ds(OWN * peer, OWN)],
            f_recv.at[:, pl.ds(pl.multiple_of(me * SENSORS + c * CHUNK, CHUNK), CHUNK), :],
            sends.at[2 + c],
            arrivals.at[2 + c],
            peer,
        )

    f_all = [
        remote(
            f_send.at[c, pl.ds(0, OWN * (PEERS - 1))],
            f_recv.at[:, pl.ds(0, CHUNK * (PEERS - 1)), :],
            sends.at[2 + c],
            arrivals.at[2 + c],
            neighbour,
        )
        for c in range(CHUNKS)
    ]
    f_self = []
    for c in range(CHUNKS):
        g = c
        for r in range(8):
            if c > 0:
                for offset in ORDER[4 * r : 4 * r + 4]:
                    f_copy(c - 1, lax.rem(me + offset, PEERS)).start()
            pair = g * 8 + r
            live = (high_row + 16 * g + r < live_rows).astype(F32)
            centered = conv[g, pl.ds(r, PATCHES, stride=8), :] - bn_mean
            normed = ((centered * bn_scale + bias) * live).astype(BF16)
            normed_ref[pair] = normed
            low = dot(normed, dft[...], NT).astype(BF16)
            low_t[pair] = dot(dft[0:16, :], normed, NT).astype(BF16)
            lhs = jnp.concatenate([normed, low], axis=1)
            for half in range(2):
                m = 16 * g + 8 * half + r
                weight = up1[m]
                rhs = jnp.concatenate(
                    [weight, zero_half, ufr[half]] if half == 0 else [zero_half, weight, ufr[half]],
                    axis=0,
                )
                value, slope = gelu_parts(dot(lhs, rhs))
                slope_ref[m] = slope
                feature = dot(down1[m], value.astype(BF16), NT)
                rows32[pl.ds(8 * half + r, CHANNELS, stride=CHUNK), :] = feature

        @pl.loop(0, CHANNELS, unroll=16)
        def _(d):
            at = pl.multiple_of(d * CHUNK, CHUNK)
            f_send[c, d] = rows32[pl.ds(at, CHUNK), :].astype(BF16)

        f_self.append(
            pltpu.make_async_copy(
                f_send.at[c, pl.ds(OWN * me, OWN)],
                f_recv.at[:, pl.ds(pl.multiple_of(me * SENSORS + c * CHUNK, CHUNK), CHUNK), :],
                self_sems.at[1 + c],
            )
        )
        f_self[-1].start()

    each_peer(me, lambda peer: f_copy(CHUNKS - 1, peer).start())

    u_self.wait()
    u_all.wait_recv()

    loads[5].wait()
    loads[6].wait()
    for dd in range(OWN):
        gh_ref[dd] = dot(down2[dd], u_recv[dd]).T

    for c in range(CHUNKS):
        f_self[c].wait()
        f_all[c].wait_recv()

    for dd in range(OWN):

        def mix(b, carry):
            pre, low = carry
            at = pl.ds(pl.multiple_of(b * 256, 256), 256)
            f = f_recv[dd, at, :]
            return pre + dot(f, up2[dd, at, :], TN), low + dot(df2_ref[:, at], f)

        pre, low = lax.fori_loop(
            0,
            SLOTS // 256,
            mix,
            (jnp.zeros((PATCHES, HIDDEN), F32), jnp.zeros((8, PATCHES), F32)),
            unroll=2,
        )
        low = low.astype(BF16)
        value, slope = gelu_parts(pre + dot(low, uf2_ref[...], TN))
        hid_ref[dd] = value.astype(BF16)
        gp2 = (gh_ref[dd] * slope).astype(BF16)
        gp2_ref[dd] = gp2
        back_ref[dd] = dot(uf2_ref[...], gp2, NT).astype(BF16)
        gu2 = dot(low, gp2)
        for t in range(2):
            tile = gu2[:, 128 * t : 128 * (t + 1)]
            part[16 + t] = tile if dd == 0 else part[16 + t] + tile

    own_block = pl.ds(OWN * me, OWN)

    def g_copy(half, peer):
        return remote(
            g_send.at[half, peer],
            g_recv.at[half, own_block],
            sends.at[6 + half],
            arrivals.at[6 + half],
            peer,
        )

    def m_copy(peer):
        return remote(m_send.at[peer], m_recv.at[own_block], sends.at[8], arrivals.at[8], peer)

    g_all = [
        remote(
            g_send.at[half, pl.ds(0, PEERS - 1)],
            g_send.at[half, pl.ds(0, PEERS - 1)],
            sends.at[6 + half],
            arrivals.at[6 + half],
            neighbour,
        )
        for half in range(HALVES)
    ]
    m_all = remote(
        m_send.at[pl.ds(0, PEERS - 1)],
        m_send.at[pl.ds(0, PEERS - 1)],
        sends.at[8],
        arrivals.at[8],
        neighbour,
    )
    g_self = [
        pltpu.make_async_copy(
            g_send.at[half, me], g_recv.at[half, own_block], self_sems.at[5 + half]
        )
        for half in range(HALVES)
    ]
    m_self = pltpu.make_async_copy(m_send.at[me], m_recv.at[own_block], self_sems.at[7])

    own_chip = me // 2
    sibling = 2 * own_chip + 1 - lax.rem(me, 2)

    def chip_at(i):
        return lax.rem(own_chip + 1 + lax.rem(i + 7, 15), 16)

    def trio(q):
        return [chip_at(3 * q + i) for i in range(3)]

    def to_trio(q, copy):
        for chip in trio(q):
            copy(2 * chip).start()
            copy(2 * chip + 1).start()

    def g_block(chip):
        at = pl.ds(pl.multiple_of(chip * 128, 128), 128)
        gd2 = []
        for dd in range(OWN):
            grad = dot(up2[dd, at, :], gp2_ref[dd], NT) + dot(df2_ref[:, at], back_ref[dd], TN)
            gd2.append(dot(back_ref[dd], f_recv[dd, at, :], NT))
            grad = grad.astype(BF16)
            for part_of in range(4):
                core, half = part_of // 2, part_of % 2
                g_send[half, 2 * chip + core, dd] = grad[BATCH * part_of : BATCH * (part_of + 1)]
        part[chip] = gd2[0] + gd2[1]

    def m_block(chip):
        at = pl.ds(pl.multiple_of(chip * 128, 128), 128)
        for dd in range(OWN):
            mix_t = dot(hid_ref[dd], down2[dd, :, at]).T.astype(BF16)
            m_send[2 * chip, dd] = mix_t[0:SENSORS]
            m_send[2 * chip + 1, dd] = mix_t[SENSORS:]

    def g_first(peer):
        return g_copy(0, peer)

    def g_second(peer):
        return g_copy(1, peer)

    for chip in trio(0):
        g_block(chip)

    @pl.loop(1, 5)
    def _(q):
        to_trio(q - 1, g_first)
        for chip in trio(q):
            g_block(chip)

    to_trio(4, g_first)
    g_block(own_chip)
    g_first(sibling).start()
    for half in range(HALVES):
        g_self[half].start()

    @pl.loop(0, 5)
    def _(q):
        to_trio(q, g_second)
        for chip in trio(q):
            m_block(chip)

    g_second(sibling).start()
    m_block(own_chip)
    each_peer(me, lambda peer: m_copy(peer).start())
    m_self.start()

    def tiles(n, ref, at):
        return remote(
            ref.at[pl.ds(0, n)], ref.at[pl.ds(0, n)], sends.at[at], arrivals.at[at], neighbour
        )

    def is_owner(device, first, last):
        return jnp.logical_and(device >= first, device < last)

    def to_owners(first, last, at):
        @pl.loop(first, last)
        def _(owner):
            @pl.when(owner != me)
            def _():
                remote(
                    part.at[owner], part_recv.at[me], sends.at[at], arrivals.at[at], owner
                ).start()

        @pl.when(is_owner(me, first, last))
        def _():
            part_recv[me] = part[me]

    def from_owners(first, last, at):
        @pl.when(is_owner(me, first, last))
        def _():
            tiles(PEERS - 1, part_recv, at).wait_recv()
            summed = jnp.sum(part_recv[...], axis=0)
            total[...] = summed
            total_recv[me] = summed
            each_peer(
                me,
                lambda peer: remote(
                    total, total_recv.at[me], sends.at[at + 1], arrivals.at[at + 1], peer
                ).start(),
            )

    def by_role(first, last, owner_act, other_act):
        owner = is_owner(me, first, last)
        pl.when(owner)(owner_act)
        pl.when(jnp.logical_not(owner))(other_act)

    def totals_arrive(first, last, at):
        by_role(
            first,
            last,
            lambda: tiles(last - first - 1, total_recv, at + 1).wait_recv(),
            lambda: tiles(last - first, total_recv, at + 1).wait_recv(),
        )

    def totals_left(first, last, at):
        def owner_act():
            tiles(last - first - 1, part, at).wait_send()
            tiles(PEERS - 1, total_recv, at + 1).wait_send()

        by_role(first, last, owner_act, lambda: tiles(last - first, part, at).wait_send())

    to_owners(0, 18, 9)

    gu1 = jnp.zeros((8, HIDDEN), F32)
    gd1 = jnp.zeros((16, 128), F32)
    for g in range(GROUPS):
        half_of = g // 2
        if g == 2:
            from_owners(0, 18, 9)
        if g % 2 == 0:
            g_self[half_of].wait()
            g_all[half_of].wait_recv()

            @pl.loop(0, CHANNELS, unroll=8)
            def _(d):
                at = pl.multiple_of(d * BATCH, BATCH)
                rows32[pl.ds(at, BATCH), :] = g_recv[half_of, d].astype(F32)

        def back(r, carry):
            gu1, gd1 = carry
            pair = g * 8 + r
            grad = jnp.concatenate(
                [
                    rows32[pl.ds(16 * (g % 2) + 8 * half + r, CHANNELS, stride=BATCH), :]
                    for half in range(2)
                ],
                axis=0,
            ).T.astype(BF16)
            gps, backs = [], []
            for half in range(2):
                m = 16 * g + 8 * half + r
                weight = down1[m]
                rhs = jnp.concatenate(
                    [weight, zero_half] if half == 0 else [zero_half, weight], axis=0
                )
                gp = (dot(grad, rhs) * slope_ref[m]).astype(BF16)
                gps.append(gp)
                backs.append(dot(uf1_ref[...], gp, NT))
            low = low_t[pair].astype(F32)
            lhs = jnp.concatenate([low[0:8], low[8:16]], axis=1).astype(BF16)
            gu1 = gu1 + dot(lhs, jnp.concatenate(gps, axis=0))
            gd1 = gd1 + dot(jnp.concatenate(backs, axis=0).astype(BF16), normed_ref[pair])
            return gu1, gd1

        gu1, gd1 = lax.fori_loop(0, 8, back, (gu1, gd1), unroll=8)

    part[18] = gu1[:, 0:128]
    part[19] = gu1[:, 128:256]
    part[20] = jnp.where(lane < CHANNELS, gd1[0:8], gd1[8:16])

    to_owners(18, TILES, 11)
    from_owners(18, TILES, 11)
    totals_arrive(0, 18, 9)
    totals_arrive(18, TILES, 11)
    total_out[...] = total_recv[0:TILES]

    m_self.wait()
    m_all.wait_recv()
    u_all.wait_send()
    st_many.wait_send()
    for sent in f_all + g_all + [m_all]:
        sent.wait_send()

    totals_left(0, 18, 9)
    totals_left(18, TILES, 11)


def finish(
    count_ref,
    series_hbm,
    received_hbm,
    total_hbm,
    mixed_hbm,
    gd1_ref,
    gu1_ref,
    gd2_ref,
    gu2_ref,
    series,
    received,
    total,
    mixed,
    rows32,
    load_sems,
    store_sems,
):
    steps = SENSORS // STEP
    loads = [
        pltpu.make_async_copy(
            received_hbm.at[:, pl.ds(step * STEP, STEP), :], received.at[step], load_sems.at[step]
        )
        for step in range(steps)
    ]
    loads.append(pltpu.make_async_copy(total_hbm, total, load_sems.at[steps]))
    blocks = [pl.ds(step * STEP, STEP) for step in range(steps)]
    series_loads = [
        pltpu.make_async_copy(
            series_hbm.at[blocks[step]], series.at[blocks[step]], load_sems.at[steps + 1 + step]
        )
        for step in range(steps)
    ]
    for step in range(steps):
        loads[step].start()
        series_loads[step].start()
    loads[steps].start()
    live_rows = count_ref[0] - lax.axis_index("var") * SENSORS
    row = lax.broadcasted_iota(jnp.int32, (STEP, PATCHES), 0)
    stores = []
    for step in range(steps):
        loads[step].wait()
        series_loads[step].wait()
        live = (row + step * STEP < live_rows).astype(F32)

        @pl.loop(0, CHANNELS, unroll=16)
        def _(d):
            rows32[pl.ds(pl.multiple_of(d * STEP, STEP), STEP), :] = (
                received[step, d].astype(F32) * live
            )

        @pl.loop(0, STEP, unroll=8)
        def _(m):
            mixed[step * STEP + m] = (
                series[step * STEP + m].astype(F32) + rows32[pl.ds(m, CHANNELS, stride=STEP), :]
            ).astype(BF16)

        stores.append(
            pltpu.make_async_copy(
                mixed.at[blocks[step]], mixed_hbm.at[blocks[step]], store_sems.at[step]
            )
        )
        stores[-1].start()

    loads[steps].wait()
    for t in range(16):
        gd2_ref[:, 128 * t : 128 * (t + 1)] = total[t]
    for t in range(2):
        gu2_ref[:, 128 * t : 128 * (t + 1)] = total[16 + t]
        gu1_ref[:, 128 * t : 128 * (t + 1)] = total[18 + t]
    both = total[20]
    gd1_ref[...] = (both + pltpu.roll(both, CHANNELS, axis=1))[:, 0:CHANNELS]
    for store in stores:
        store.wait()


def body(
    series,
    sensor_total_count,
    depthwise_weight,
    batchnorm_gain,
    batchnorm_bias,
    channel_up_weight,
    channel_down_weight,
    down_factor1,
    up_factor1,
    sensor_up_weight,
    sensor_down_weight,
    down_factor2,
    up_factor2,
    upstream,
):
    vmem = pl.BlockSpec(memory_space=pltpu.VMEM)
    hbm = pl.BlockSpec(memory_space=pltpu.HBM)
    rows = PATCHES * 8
    dma = pltpu.SemaphoreType.DMA
    received, total = pl.pallas_call(
        kernel,
        out_shape=(
            jax.ShapeDtypeStruct((CHANNELS, SENSORS, PATCHES), BF16),
            jax.ShapeDtypeStruct((TILES, 8, 128), F32),
        ),
        in_specs=[pl.BlockSpec(memory_space=pltpu.SMEM)] + [vmem] * 6 + [hbm] * 7,
        out_specs=(hbm, vmem),
        scratch_shapes=[
            pltpu.VMEM((SENSORS, CHANNELS, PATCHES), BF16),
            pltpu.VMEM((TAPS, SENSORS, CHANNELS), BF16),
            pltpu.VMEM((SENSORS, CHANNELS, HIDDEN), BF16),
            pltpu.VMEM((SENSORS, CHANNELS, HIDDEN), BF16),
            pltpu.VMEM((OWN, SLOTS, HIDDEN), BF16),
            pltpu.VMEM((OWN, HIDDEN, SLOTS), BF16),
            pltpu.VMEM((SENSORS, CHANNELS, PATCHES), BF16),
            pltpu.VMEM((GROUPS, PADDED * 8, 128), F32),
            pltpu.VMEM((TAPS, GROUPS, 8, 128), F32),
            pltpu.VMEM((GROUPS, rows, 128), F32),
            pltpu.VMEM((SENSORS * CHANNELS, PATCHES), F32),
            pltpu.VMEM((SENSORS // 2, PATCHES, 128), BF16),
            pltpu.VMEM((SENSORS // 2, 16, PATCHES), BF16),
            pltpu.VMEM((SENSORS, PATCHES, HIDDEN), F32),
            pltpu.VMEM((CHANNELS, SENSORS, PATCHES), BF16),
            pltpu.VMEM((OWN, SLOTS, PATCHES), BF16),
            pltpu.VMEM((CHUNKS, CHANNELS, CHUNK, PATCHES), BF16),
            pltpu.VMEM((OWN, SLOTS, PATCHES), BF16),
            pltpu.VMEM((HALVES, PEERS, OWN, BATCH, PATCHES), BF16),
            pltpu.VMEM((HALVES, CHANNELS, BATCH, PATCHES), BF16),
            pltpu.VMEM((PEERS, OWN, SENSORS, PATCHES), BF16),
            pltpu.VMEM((8, 128), F32),
            pltpu.VMEM((PEERS, 8, 128), F32),
            pltpu.VMEM((128, 128), BF16),
            pltpu.VMEM((2, 128, HIDDEN), BF16),
            pltpu.VMEM((OWN, PATCHES, HIDDEN), F32),
            pltpu.VMEM((OWN, PATCHES, HIDDEN), BF16),
            pltpu.VMEM((OWN, PATCHES, HIDDEN), BF16),
            pltpu.VMEM((OWN, 8, PATCHES), BF16),
            pltpu.VMEM((PEERS, 8, 128), F32),
            pltpu.VMEM((PEERS, 8, 128), F32),
            pltpu.VMEM((8, 128), F32),
            pltpu.VMEM((PEERS, 8, 128), F32),
            dma((7,)),
            dma((8,)),
            dma((13,)),
            dma((13,)),
        ],
        compiler_params=pltpu.CompilerParams(
            collective_id=0, has_side_effects=True, vmem_limit_bytes=60 * 1024 * 1024
        ),
        cost_estimate=pl.CostEstimate(
            flops=2_000_000_000, bytes_accessed=12_000_000, transcendentals=2_200_000
        ),
    )(
        sensor_total_count,
        batchnorm_gain.reshape(1, CHANNELS),
        batchnorm_bias.reshape(1, CHANNELS),
        down_factor1.T,
        up_factor1,
        down_factor2.T,
        up_factor2,
        series[0],
        jnp.transpose(depthwise_weight, (2, 0, 1)),
        channel_up_weight,
        jnp.transpose(channel_down_weight, (0, 2, 1)),
        sensor_up_weight,
        sensor_down_weight,
        upstream[0],
    )
    mixed, gd1, gu1, gd2, gu2 = pl.pallas_call(
        finish,
        out_shape=(
            jax.ShapeDtypeStruct((SENSORS, CHANNELS, PATCHES), BF16),
            jax.ShapeDtypeStruct((8, CHANNELS), F32),
            jax.ShapeDtypeStruct((8, HIDDEN), F32),
            jax.ShapeDtypeStruct((8, SLOTS), F32),
            jax.ShapeDtypeStruct((8, HIDDEN), F32),
        ),
        in_specs=[pl.BlockSpec(memory_space=pltpu.SMEM), hbm, hbm, hbm],
        out_specs=(hbm, vmem, vmem, vmem, vmem),
        scratch_shapes=[
            pltpu.VMEM((SENSORS, CHANNELS, PATCHES), BF16),
            pltpu.VMEM((SENSORS // STEP, CHANNELS, STEP, PATCHES), BF16),
            pltpu.VMEM((TILES, 8, 128), F32),
            pltpu.VMEM((SENSORS, CHANNELS, PATCHES), BF16),
            pltpu.VMEM((STEP * CHANNELS, PATCHES), F32),
            dma((2 * (SENSORS // STEP) + 1,)),
            dma((SENSORS // STEP,)),
        ],
        compiler_params=pltpu.CompilerParams(vmem_limit_bytes=60 * 1024 * 1024),
    )(sensor_total_count, series[0], received, total)
    return mixed[None], gd1.T, gu1, gd2.T, gu2


def solution(mesh):
    placed = (
        P("grp", "var", None, None),
        P("grp"),
        P("var", None, None),
        P(),
        P(),
        P("var", None, None),
        P("var", None, None),
        P(),
        P(),
        P("var", None, None),
        P("var", None, None),
        P(),
        P(),
        P("grp", "var", None, None),
    )
    return jax.shard_map(
        body,
        mesh=mesh,
        in_specs=placed,
        out_specs=(
            P("grp", "var", None, None),
            P("grp", None),
            P("grp", None),
            P("grp", None),
            P("grp", None),
        ),
        check_vma=False,
    )
```

```python
import jax
import jax.numpy as jnp
from jax import lax
from jax.experimental import pallas as pl
from jax.experimental.pallas import tpu as pltpu
from jax.sharding import PartitionSpec as P

F32 = jnp.float32
BF16 = jnp.bfloat16
MESH = pl.DeviceIdType.MESH

tanh_scale = 0.7978845608028654
cubic_term = 0.044715

PEERS = 32
SENSORS = 64
CHANNELS = 64
PATCHES = 128
TAPS = 51
HALF = TAPS // 2
GROUPS = 4
PADDED = PATCHES + 2 * HALF
SLOTS = PEERS * SENSORS
HIDDEN = 256
OWN = 2
CHUNKS = 2
CHUNK = SENSORS // CHUNKS
HALVES = 2
BATCH = SENSORS // HALVES
TILES = 21
STEP = 16
BLOCK = 16


def gelu_parts(v):
    square = v * v
    half = 0.5 * jnp.tanh(v * (tanh_scale + (tanh_scale * cubic_term) * square)) + 0.5
    value = v * half
    slope = half + (value * (1.0 - half)) * (
        2.0 * tanh_scale + (6.0 * tanh_scale * cubic_term) * square
    )
    return value, slope


def dot(a, b, contract=((1,), (0,))):
    return lax.dot_general(a, b, (contract, ((), ())), preferred_element_type=F32)


NT = ((1,), (1,))
TN = ((0,), (0,))


def each_peer(me, act):
    for first, last, unroll in ((16, PEERS, 4), (1, 16, 5)):

        @pl.loop(first, last, unroll=unroll)
        def _(i):
            act(lax.rem(me + i, PEERS))


def kernel(
    count_ref,
    gain_ref,
    bias_ref,
    df1_ref,
    uf1_ref,
    df2_ref,
    uf2_ref,
    series_hbm,
    taps_hbm,
    up1_hbm,
    down1_hbm,
    up2_hbm,
    down2_hbm,
    upstream_hbm,
    m_recv,
    total_out,
    series,
    taps,
    up1,
    down1,
    up2,
    down2,
    upstream,
    padded,
    packed_taps,
    conv,
    rows32,
    normed_ref,
    low_t,
    slope_ref,
    u_send,
    u_recv,
    f_send,
    f_recv,
    g_send,
    g_recv,
    m_send,
    st_send,
    st_recv,
    dft,
    ufr,
    gh_ref,
    hid_ref,
    gp2_ref,
    back_ref,
    part,
    part_recv,
    total,
    total_recv,
    load_sems,
    self_sems,
    sends,
    arrivals,
):
    me = lax.axis_index("var")
    limit = count_ref[0]
    live_rows = limit - me * SENSORS

    def remote(src, dst, ssem, rsem, peer):
        return pltpu.make_async_remote_copy(
            src_ref=src,
            dst_ref=dst,
            send_sem=ssem,
            recv_sem=rsem,
            device_id={"var": peer},
            device_id_type=MESH,
        )

    loads = [
        pltpu.make_async_copy(src, dst, load_sems.at[i])
        for i, (src, dst) in enumerate(
            (
                (upstream_hbm, upstream),
                (series_hbm, series),
                (taps_hbm, taps),
                (up1_hbm, up1),
                (down1_hbm, down1),
                (down2_hbm, down2),
                (up2_hbm, up2),
            )
        )
    ]
    for load in loads[:3]:
        load.start()

    barrier = pltpu.get_barrier_semaphore()

    def greet(peer):
        pl.semaphore_signal(barrier, inc=1, device_id={"var": peer}, device_id_type=MESH)

    each_peer(me, greet)

    loads[0].wait()
    row_index = lax.broadcasted_iota(jnp.int32, (SENSORS, PATCHES), 0)
    live_sensor = (row_index < live_rows).astype(F32)

    @pl.loop(0, SENSORS, unroll=8)
    def _(m):
        rows32[pl.ds(m, CHANNELS, stride=SENSORS), :] = upstream[m].astype(F32)

    @pl.loop(0, CHANNELS, unroll=8)
    def _(d):
        at = pl.multiple_of(d * SENSORS, SENSORS)
        u_send[d] = (rows32[pl.ds(at, SENSORS), :] * live_sensor).astype(BF16)

    df1 = df1_ref[...].astype(F32)
    zero8 = jnp.zeros((8, CHANNELS), F32)
    dft[...] = jnp.concatenate(
        [
            jnp.concatenate([df1, zero8], axis=1),
            jnp.concatenate([zero8, df1], axis=1),
            jnp.zeros((112, 128), F32),
        ],
        axis=0,
    ).astype(BF16)
    uf1_32 = uf1_ref[...].astype(F32)
    ufr[0] = jnp.concatenate([uf1_32, jnp.zeros((120, HIDDEN), F32)], axis=0).astype(BF16)
    ufr[1] = jnp.concatenate(
        [jnp.zeros((8, HIDDEN), F32), uf1_32, jnp.zeros((112, HIDDEN), F32)], axis=0
    ).astype(BF16)

    loads[1].wait()
    loads[2].wait()
    for load in loads[3:]:
        load.start()
    padded[:, 0 : HALF * 8, :] = jnp.zeros((GROUPS, HALF * 8, 128), F32)
    padded[:, (HALF + PATCHES) * 8 : PADDED * 8, :] = jnp.zeros((GROUPS, HALF * 8, 128), F32)

    for g in range(GROUPS):

        @pl.loop(0, 8, unroll=8)
        def _(r):
            both = jnp.concatenate(
                [series[16 * g + r].astype(F32), series[16 * g + 8 + r].astype(F32)], axis=0
            )
            padded[g, pl.ds(HALF * 8 + r, PATCHES, stride=8), :] = both.T

    @pl.loop(0, TAPS, unroll=3)
    def _(k):
        row = taps[k].astype(F32)
        for g in range(GROUPS):
            packed_taps[k, g] = jnp.concatenate(
                [row[16 * g : 16 * g + 8], row[16 * g + 8 : 16 * g + 16]], axis=1
            )

    pl.semaphore_wait(barrier, PEERS - 1)
    mine = pl.ds(pl.multiple_of(me * SENSORS, SENSORS), SENSORS)
    neighbour = lax.rem(me + 1, PEERS)

    def u_start(peer):
        remote(
            u_send.at[pl.ds(OWN * peer, OWN)], u_recv.at[:, mine, :], sends.at[0], arrivals.at[0], peer
        ).start()

    each_peer(me, u_start)
    u_self = pltpu.make_async_copy(
        u_send.at[pl.ds(OWN * me, OWN)], u_recv.at[:, mine, :], self_sems.at[0]
    )
    u_self.start()
    u_all = remote(
        u_send.at[pl.ds(0, OWN * (PEERS - 1))],
        u_recv.at[:, pl.ds(0, SENSORS * (PEERS - 1)), :],
        sends.at[0],
        arrivals.at[0],
        neighbour,
    )

    sub = lax.broadcasted_iota(jnp.int32, (8, 128), 0)
    lane = lax.broadcasted_iota(jnp.int32, (8, 128), 1)
    high = (lane >= CHANNELS).astype(jnp.int32) * 8

    def group_mask(g):
        return (sub + high + 16 * g < live_rows).astype(F32)

    def conv_group(g, sums):
        def conv_block(nb, acc_sum):
            base = pl.multiple_of(nb * (BLOCK * 8), BLOCK * 8)
            acc = [None] * BLOCK
            tap = {}
            for j in range(BLOCK + TAPS - 1):
                x = padded[g, pl.ds(base + 8 * j, 8), :]
                if j < TAPS:
                    tap[j] = packed_taps[j, g]
                for i in range(max(0, j - TAPS + 1), min(BLOCK - 1, j) + 1):
                    term = tap[j - i] * x
                    acc[i] = term if acc[i] is None else acc[i] + term
            for i in range(BLOCK):
                conv[g, pl.ds(base + 8 * i, 8), :] = acc[i]
                acc_sum = acc_sum + acc[i]
            return acc_sum

        group_sum = lax.fori_loop(0, PATCHES // BLOCK, conv_block, jnp.zeros((8, 128), F32))
        return sums + group_sum * group_mask(g)

    sums = lax.fori_loop(0, GROUPS, conv_group, jnp.zeros((8, 128), F32))

    def fold(v):
        v = jnp.sum(v, axis=0, keepdims=True)
        return v + pltpu.roll(v, CHANNELS, axis=1)

    sum_row = fold(sums)
    own_count = jnp.clip(live_rows, 0, SENSORS).astype(F32) * PATCHES
    own_mean = sum_row / jnp.maximum(own_count, 1.0)

    def square_group(g, squares):
        def block(b, acc):
            at = pl.multiple_of(b * 128, 128)
            c = conv[g, pl.ds(at, 128), :] - own_mean
            return acc + jnp.sum((c * c).reshape(16, 8, 128), axis=0)

        group = lax.fori_loop(0, 8, block, jnp.zeros((8, 128), F32))
        return squares + group * group_mask(g)

    square_row = fold(lax.fori_loop(0, GROUPS, square_group, jnp.zeros((8, 128), F32)))
    stats = jnp.where(
        sub == 0,
        sum_row,
        jnp.where(sub == 1, square_row, jnp.where(sub == 2, own_mean, own_count)),
    )
    st_send[...] = stats
    st_recv[me] = stats

    each_peer(
        me,
        lambda peer: remote(
            st_send, st_recv.at[me], sends.at[1], arrivals.at[1], peer
        ).start(),
    )

    st_many = remote(
        st_recv.at[pl.ds(0, PEERS - 1)],
        st_recv.at[pl.ds(0, PEERS - 1)],
        sends.at[1],
        arrivals.at[1],
        neighbour,
    )
    st_many.wait_recv()
    st_all = st_recv[...]
    st_sum = jnp.sum(st_all, axis=0)
    live_total = limit.astype(F32) * PATCHES
    bn_mean = st_sum[0:1] / live_total
    means = st_all[:, 2:3, :] - bn_mean[None]
    shift_squares = jnp.sum(st_all[:, 3:4, :] * means * means, axis=0)
    spread = (st_sum[1:2] + shift_squares) / live_total
    gain = jnp.concatenate([gain_ref[...], gain_ref[...]], axis=1)
    bias = jnp.concatenate([bias_ref[...], bias_ref[...]], axis=1)
    bn_scale = gain * lax.rsqrt(spread + 1e-05)

    loads[3].wait()
    loads[4].wait()
    zero_half = jnp.zeros((CHANNELS, HIDDEN), BF16)
    lane_row = lax.broadcasted_iota(jnp.int32, (1, 128), 1)
    high_row = (lane_row >= CHANNELS).astype(jnp.int32) * 8

    def f_copy(c, peer):
        return remote(
            f_send.at[c, pl.ds(OWN * peer, OWN)],
            f_recv.at[:, pl.ds(pl.multiple_of(me * SENSORS + c * CHUNK, CHUNK), CHUNK), :],
            sends.at[2 + c],
            arrivals.at[2 + c],
            peer,
        )

    f_all = [
        remote(
            f_send.at[c, pl.ds(0, OWN * (PEERS - 1))],
            f_recv.at[:, pl.ds(0, CHUNK * (PEERS - 1)), :],
            sends.at[2 + c],
            arrivals.at[2 + c],
            neighbour,
        )
        for c in range(CHUNKS)
    ]
    f_self = []
    for c in range(CHUNKS):
        for gl in range(GROUPS // CHUNKS):
            g = c * (GROUPS // CHUNKS) + gl

            @pl.loop(0, 8, unroll=8)
            def _(r):
                pair = g * 8 + r
                live = (high_row + 16 * g + r < live_rows).astype(F32)
                centered = conv[g, pl.ds(r, PATCHES, stride=8), :] - bn_mean
                normed = ((centered * bn_scale + bias) * live).astype(BF16)
                normed_ref[pair] = normed
                low = dot(normed, dft[...], NT).astype(BF16)
                low_t[pair] = dot(dft[0:16, :], normed, NT).astype(BF16)
                lhs = jnp.concatenate([normed, low], axis=1)
                for half in range(2):
                    m = 16 * g + 8 * half + r
                    weight = up1[m]
                    rhs = jnp.concatenate(
                        [weight, zero_half, ufr[half]] if half == 0 else [zero_half, weight, ufr[half]],
                        axis=0,
                    )
                    value, slope = gelu_parts(dot(lhs, rhs))
                    slope_ref[m] = slope
                    feature = dot(down1[m], value.astype(BF16), NT)
                    rows32[pl.ds(16 * gl + 8 * half + r, CHANNELS, stride=CHUNK), :] = feature

        @pl.loop(0, CHANNELS, unroll=8)
        def _(d):
            at = pl.multiple_of(d * CHUNK, CHUNK)
            f_send[c, d] = rows32[pl.ds(at, CHUNK), :].astype(BF16)

        each_peer(me, lambda peer: f_copy(c, peer).start())

        f_self.append(
            pltpu.make_async_copy(
                f_send.at[c, pl.ds(OWN * me, OWN)],
                f_recv.at[:, pl.ds(pl.multiple_of(me * SENSORS + c * CHUNK, CHUNK), CHUNK), :],
                self_sems.at[1 + c],
            )
        )
        f_self[-1].start()

    u_self.wait()
    u_all.wait_recv()

    loads[5].wait()
    loads[6].wait()
    for dd in range(OWN):
        gh_ref[dd] = dot(down2[dd], u_recv[dd]).T

    for c in range(CHUNKS):
        f_self[c].wait()
        f_all[c].wait_recv()

    for dd in range(OWN):

        def mix(b, carry):
            pre, low = carry
            at = pl.ds(pl.multiple_of(b * 256, 256), 256)
            f = f_recv[dd, at, :]
            return pre + dot(f, up2[dd, at, :], TN), low + dot(df2_ref[:, at], f)

        pre, low = lax.fori_loop(
            0,
            SLOTS // 256,
            mix,
            (jnp.zeros((PATCHES, HIDDEN), F32), jnp.zeros((8, PATCHES), F32)),
            unroll=2,
        )
        low = low.astype(BF16)
        value, slope = gelu_parts(pre + dot(low, uf2_ref[...], TN))
        hid_ref[dd] = value.astype(BF16)
        gp2 = (gh_ref[dd] * slope).astype(BF16)
        gp2_ref[dd] = gp2
        back_ref[dd] = dot(uf2_ref[...], gp2, NT).astype(BF16)
        gu2 = dot(low, gp2)
        for t in range(2):
            tile = gu2[:, 128 * t : 128 * (t + 1)]
            part[16 + t] = tile if dd == 0 else part[16 + t] + tile

    own_block = pl.ds(OWN * me, OWN)

    def g_copy(half, peer):
        return remote(
            g_send.at[half, peer],
            g_recv.at[half, own_block],
            sends.at[6 + half],
            arrivals.at[6 + half],
            peer,
        )

    def m_copy(peer):
        return remote(m_send.at[peer], m_recv.at[own_block], sends.at[8], arrivals.at[8], peer)

    g_all = [
        remote(
            g_send.at[half, pl.ds(0, PEERS - 1)],
            g_send.at[half, pl.ds(0, PEERS - 1)],
            sends.at[6 + half],
            arrivals.at[6 + half],
            neighbour,
        )
        for half in range(HALVES)
    ]
    m_all = remote(
        m_send.at[pl.ds(0, PEERS - 1)],
        m_send.at[pl.ds(0, PEERS - 1)],
        sends.at[8],
        arrivals.at[8],
        neighbour,
    )
    g_self = [
        pltpu.make_async_copy(
            g_send.at[half, me], g_recv.at[half, own_block], self_sems.at[5 + half]
        )
        for half in range(HALVES)
    ]
    m_self = pltpu.make_async_copy(m_send.at[me], m_recv.at[own_block], self_sems.at[7])

    own_chip = me // 2
    sibling = 2 * own_chip + 1 - lax.rem(me, 2)

    def chip_at(i):
        return lax.rem(own_chip + 1 + lax.rem(i + 7, 15), 16)

    def each_chip(act, send):
        @pl.loop(0, 5)
        def _(q):
            chips = [chip_at(3 * q + i) for i in range(3)]
            if act is not None:
                for chip in chips:
                    act(chip)
            for chip in chips:
                send(2 * chip)
                send(2 * chip + 1)

        if act is not None:
            act(own_chip)
        send(sibling)

    def g_block(chip):
        at = pl.ds(pl.multiple_of(chip * 128, 128), 128)
        gd2 = []
        for dd in range(OWN):
            grad = dot(up2[dd, at, :], gp2_ref[dd], NT) + dot(df2_ref[:, at], back_ref[dd], TN)
            gd2.append(dot(back_ref[dd], f_recv[dd, at, :], NT))
            grad = grad.astype(BF16)
            for part_of in range(4):
                core, half = part_of // 2, part_of % 2
                g_send[half, 2 * chip + core, dd] = grad[BATCH * part_of : BATCH * (part_of + 1)]
        part[chip] = gd2[0] + gd2[1]

    def m_block(chip):
        at = pl.ds(pl.multiple_of(chip * 128, 128), 128)
        for dd in range(OWN):
            mix_t = dot(hid_ref[dd], down2[dd, :, at]).T.astype(BF16)
            m_send[2 * chip, dd] = mix_t[0:SENSORS]
            m_send[2 * chip + 1, dd] = mix_t[SENSORS:]

    each_chip(g_block, lambda peer: g_copy(0, peer).start())
    each_chip(None, lambda peer: g_copy(1, peer).start())
    for half in range(HALVES):
        g_self[half].start()

    def tiles(n, ref, at):
        return remote(
            ref.at[pl.ds(0, n)], ref.at[pl.ds(0, n)], sends.at[at], arrivals.at[at], neighbour
        )

    def is_owner(device, first, last):
        return jnp.logical_and(device >= first, device < last)

    def to_owners(first, last, at):
        @pl.loop(first, last)
        def _(owner):
            @pl.when(owner != me)
            def _():
                remote(
                    part.at[owner], part_recv.at[me], sends.at[at], arrivals.at[at], owner
                ).start()

        @pl.when(is_owner(me, first, last))
        def _():
            part_recv[me] = part[me]

    def from_owners(first, last, at):
        @pl.when(is_owner(me, first, last))
        def _():
            tiles(PEERS - 1, part_recv, at).wait_recv()
            summed = jnp.sum(part_recv[...], axis=0)
            total[...] = summed
            total_recv[me] = summed
            each_peer(
                me,
                lambda peer: remote(
                    total, total_recv.at[me], sends.at[at + 1], arrivals.at[at + 1], peer
                ).start(),
            )

    def by_role(first, last, owner_act, other_act):
        owner = is_owner(me, first, last)
        pl.when(owner)(owner_act)
        pl.when(jnp.logical_not(owner))(other_act)

    def totals_arrive(first, last, at):
        by_role(
            first,
            last,
            lambda: tiles(last - first - 1, total_recv, at + 1).wait_recv(),
            lambda: tiles(last - first, total_recv, at + 1).wait_recv(),
        )

    def totals_left(first, last, at):
        def owner_act():
            tiles(last - first - 1, part, at).wait_send()
            tiles(PEERS - 1, total_recv, at + 1).wait_send()

        by_role(first, last, owner_act, lambda: tiles(last - first, part, at).wait_send())

    each_chip(m_block, lambda peer: m_copy(peer).start())
    m_self.start()
    to_owners(0, 18, 9)

    gu1 = jnp.zeros((8, HIDDEN), F32)
    gd1 = jnp.zeros((16, 128), F32)
    for g in range(GROUPS):
        half_of = g // 2
        if g == 2:
            from_owners(0, 18, 9)
        if g % 2 == 0:
            g_self[half_of].wait()
            g_all[half_of].wait_recv()

            @pl.loop(0, CHANNELS, unroll=8)
            def _(d):
                at = pl.multiple_of(d * BATCH, BATCH)
                rows32[pl.ds(at, BATCH), :] = g_recv[half_of, d].astype(F32)

        def back(r, carry):
            gu1, gd1 = carry
            pair = g * 8 + r
            grad = jnp.concatenate(
                [
                    rows32[pl.ds(16 * (g % 2) + 8 * half + r, CHANNELS, stride=BATCH), :]
                    for half in range(2)
                ],
                axis=0,
            ).T.astype(BF16)
            gps, backs = [], []
            for half in range(2):
                m = 16 * g + 8 * half + r
                weight = down1[m]
                rhs = jnp.concatenate(
                    [weight, zero_half] if half == 0 else [zero_half, weight], axis=0
                )
                gp = (dot(grad, rhs) * slope_ref[m]).astype(BF16)
                gps.append(gp)
                backs.append(dot(uf1_ref[...], gp, NT))
            low = low_t[pair].astype(F32)
            lhs = jnp.concatenate([low[0:8], low[8:16]], axis=1).astype(BF16)
            gu1 = gu1 + dot(lhs, jnp.concatenate(gps, axis=0))
            gd1 = gd1 + dot(jnp.concatenate(backs, axis=0).astype(BF16), normed_ref[pair])
            return gu1, gd1

        gu1, gd1 = lax.fori_loop(0, 8, back, (gu1, gd1), unroll=8)

    part[18] = gu1[:, 0:128]
    part[19] = gu1[:, 128:256]
    part[20] = jnp.where(lane < CHANNELS, gd1[0:8], gd1[8:16])

    to_owners(18, TILES, 11)
    from_owners(18, TILES, 11)
    totals_arrive(0, 18, 9)
    totals_arrive(18, TILES, 11)
    total_out[...] = total_recv[0:TILES]

    m_self.wait()
    m_all.wait_recv()
    u_all.wait_send()
    st_many.wait_send()
    for sent in f_all + g_all + [m_all]:
        sent.wait_send()

    totals_left(0, 18, 9)
    totals_left(18, TILES, 11)


def finish(
    count_ref,
    series_hbm,
    received_hbm,
    total_hbm,
    mixed_hbm,
    gd1_ref,
    gu1_ref,
    gd2_ref,
    gu2_ref,
    series,
    received,
    total,
    mixed,
    rows32,
    load_sems,
    store_sems,
):
    steps = SENSORS // STEP
    loads = [
        pltpu.make_async_copy(
            received_hbm.at[:, pl.ds(step * STEP, STEP), :], received.at[step], load_sems.at[step]
        )
        for step in range(steps)
    ]
    loads.append(pltpu.make_async_copy(total_hbm, total, load_sems.at[steps]))
    blocks = [pl.ds(step * STEP, STEP) for step in range(steps)]
    series_loads = [
        pltpu.make_async_copy(
            series_hbm.at[blocks[step]], series.at[blocks[step]], load_sems.at[steps + 1 + step]
        )
        for step in range(steps)
    ]
    for step in range(steps):
        loads[step].start()
        series_loads[step].start()
    loads[steps].start()
    live_rows = count_ref[0] - lax.axis_index("var") * SENSORS
    row = lax.broadcasted_iota(jnp.int32, (STEP, PATCHES), 0)
    stores = []
    for step in range(steps):
        loads[step].wait()
        series_loads[step].wait()
        live = (row + step * STEP < live_rows).astype(F32)

        @pl.loop(0, CHANNELS, unroll=16)
        def _(d):
            rows32[pl.ds(pl.multiple_of(d * STEP, STEP), STEP), :] = (
                received[step, d].astype(F32) * live
            )

        @pl.loop(0, STEP, unroll=8)
        def _(m):
            mixed[step * STEP + m] = (
                series[step * STEP + m].astype(F32) + rows32[pl.ds(m, CHANNELS, stride=STEP), :]
            ).astype(BF16)

        stores.append(
            pltpu.make_async_copy(
                mixed.at[blocks[step]], mixed_hbm.at[blocks[step]], store_sems.at[step]
            )
        )
        stores[-1].start()

    loads[steps].wait()
    for t in range(16):
        gd2_ref[:, 128 * t : 128 * (t + 1)] = total[t]
    for t in range(2):
        gu2_ref[:, 128 * t : 128 * (t + 1)] = total[16 + t]
        gu1_ref[:, 128 * t : 128 * (t + 1)] = total[18 + t]
    both = total[20]
    gd1_ref[...] = (both + pltpu.roll(both, CHANNELS, axis=1))[:, 0:CHANNELS]
    for store in stores:
        store.wait()


def body(
    series,
    sensor_total_count,
    depthwise_weight,
    batchnorm_gain,
    batchnorm_bias,
    channel_up_weight,
    channel_down_weight,
    down_factor1,
    up_factor1,
    sensor_up_weight,
    sensor_down_weight,
    down_factor2,
    up_factor2,
    upstream,
):
    vmem = pl.BlockSpec(memory_space=pltpu.VMEM)
    hbm = pl.BlockSpec(memory_space=pltpu.HBM)
    rows = PATCHES * 8
    dma = pltpu.SemaphoreType.DMA
    received, total = pl.pallas_call(
        kernel,
        out_shape=(
            jax.ShapeDtypeStruct((CHANNELS, SENSORS, PATCHES), BF16),
            jax.ShapeDtypeStruct((TILES, 8, 128), F32),
        ),
        in_specs=[pl.BlockSpec(memory_space=pltpu.SMEM)] + [vmem] * 6 + [hbm] * 7,
        out_specs=(hbm, vmem),
        scratch_shapes=[
            pltpu.VMEM((SENSORS, CHANNELS, PATCHES), BF16),
            pltpu.VMEM((TAPS, SENSORS, CHANNELS), BF16),
            pltpu.VMEM((SENSORS, CHANNELS, HIDDEN), BF16),
            pltpu.VMEM((SENSORS, CHANNELS, HIDDEN), BF16),
            pltpu.VMEM((OWN, SLOTS, HIDDEN), BF16),
            pltpu.VMEM((OWN, HIDDEN, SLOTS), BF16),
            pltpu.VMEM((SENSORS, CHANNELS, PATCHES), BF16),
            pltpu.VMEM((GROUPS, PADDED * 8, 128), F32),
            pltpu.VMEM((TAPS, GROUPS, 8, 128), F32),
            pltpu.VMEM((GROUPS, rows, 128), F32),
            pltpu.VMEM((SENSORS * CHANNELS, PATCHES), F32),
            pltpu.VMEM((SENSORS // 2, PATCHES, 128), BF16),
            pltpu.VMEM((SENSORS // 2, 16, PATCHES), BF16),
            pltpu.VMEM((SENSORS, PATCHES, HIDDEN), F32),
            pltpu.VMEM((CHANNELS, SENSORS, PATCHES), BF16),
            pltpu.VMEM((OWN, SLOTS, PATCHES), BF16),
            pltpu.VMEM((CHUNKS, CHANNELS, CHUNK, PATCHES), BF16),
            pltpu.VMEM((OWN, SLOTS, PATCHES), BF16),
            pltpu.VMEM((HALVES, PEERS, OWN, BATCH, PATCHES), BF16),
            pltpu.VMEM((HALVES, CHANNELS, BATCH, PATCHES), BF16),
            pltpu.VMEM((PEERS, OWN, SENSORS, PATCHES), BF16),
            pltpu.VMEM((8, 128), F32),
            pltpu.VMEM((PEERS, 8, 128), F32),
            pltpu.VMEM((128, 128), BF16),
            pltpu.VMEM((2, 128, HIDDEN), BF16),
            pltpu.VMEM((OWN, PATCHES, HIDDEN), F32),
            pltpu.VMEM((OWN, PATCHES, HIDDEN), BF16),
            pltpu.VMEM((OWN, PATCHES, HIDDEN), BF16),
            pltpu.VMEM((OWN, 8, PATCHES), BF16),
            pltpu.VMEM((PEERS, 8, 128), F32),
            pltpu.VMEM((PEERS, 8, 128), F32),
            pltpu.VMEM((8, 128), F32),
            pltpu.VMEM((PEERS, 8, 128), F32),
            dma((7,)),
            dma((8,)),
            dma((13,)),
            dma((13,)),
        ],
        compiler_params=pltpu.CompilerParams(
            collective_id=0, has_side_effects=True, vmem_limit_bytes=60 * 1024 * 1024
        ),
        cost_estimate=pl.CostEstimate(
            flops=2_000_000_000, bytes_accessed=12_000_000, transcendentals=2_200_000
        ),
    )(
        sensor_total_count,
        batchnorm_gain.reshape(1, CHANNELS),
        batchnorm_bias.reshape(1, CHANNELS),
        down_factor1.T,
        up_factor1,
        down_factor2.T,
        up_factor2,
        series[0],
        jnp.transpose(depthwise_weight, (2, 0, 1)),
        channel_up_weight,
        jnp.transpose(channel_down_weight, (0, 2, 1)),
        sensor_up_weight,
        sensor_down_weight,
        upstream[0],
    )
    mixed, gd1, gu1, gd2, gu2 = pl.pallas_call(
        finish,
        out_shape=(
            jax.ShapeDtypeStruct((SENSORS, CHANNELS, PATCHES), BF16),
            jax.ShapeDtypeStruct((8, CHANNELS), F32),
            jax.ShapeDtypeStruct((8, HIDDEN), F32),
            jax.ShapeDtypeStruct((8, SLOTS), F32),
            jax.ShapeDtypeStruct((8, HIDDEN), F32),
        ),
        in_specs=[pl.BlockSpec(memory_space=pltpu.SMEM), hbm, hbm, hbm],
        out_specs=(hbm, vmem, vmem, vmem, vmem),
        scratch_shapes=[
            pltpu.VMEM((SENSORS, CHANNELS, PATCHES), BF16),
            pltpu.VMEM((SENSORS // STEP, CHANNELS, STEP, PATCHES), BF16),
            pltpu.VMEM((TILES, 8, 128), F32),
            pltpu.VMEM((SENSORS, CHANNELS, PATCHES), BF16),
            pltpu.VMEM((STEP * CHANNELS, PATCHES), F32),
            dma((2 * (SENSORS // STEP) + 1,)),
            dma((SENSORS // STEP,)),
        ],
        compiler_params=pltpu.CompilerParams(vmem_limit_bytes=60 * 1024 * 1024),
    )(sensor_total_count, series[0], received, total)
    return mixed[None], gd1.T, gu1, gd2.T, gu2


def solution(mesh):
    placed = (
        P("grp", "var", None, None),
        P("grp"),
        P("var", None, None),
        P(),
        P(),
        P("var", None, None),
        P("var", None, None),
        P(),
        P(),
        P("var", None, None),
        P("var", None, None),
        P(),
        P(),
        P("grp", "var", None, None),
    )
    return jax.shard_map(
        body,
        mesh=mesh,
        in_specs=placed,
        out_specs=(
            P("grp", "var", None, None),
            P("grp", None),
            P("grp", None),
            P("grp", None),
            P("grp", None),
        ),
        check_vma=False,
    )
```

```python
import jax
import jax.numpy as jnp
from jax import lax
from jax.experimental import pallas as pl
from jax.experimental.pallas import tpu as pltpu
from jax.sharding import PartitionSpec as P

F32 = jnp.float32
BF16 = jnp.bfloat16
MESH = pl.DeviceIdType.MESH

tanh_scale = 0.7978845608028654
cubic_term = 0.044715

PEERS = 32
SENSORS = 64
CHANNELS = 64
PATCHES = 128
TAPS = 51
HALF = TAPS // 2
GROUPS = 4
PADDED = PATCHES + 2 * HALF
SLOTS = PEERS * SENSORS
HIDDEN = 256
OWN = 2
CHUNKS = 4
CHUNK = SENSORS // CHUNKS
HALVES = 2
BATCH = SENSORS // HALVES
TILES = 21
STEP = 16
BLOCK = 16


def gelu_parts(v):
    square = v * v
    half = 0.5 * jnp.tanh(v * (tanh_scale + (tanh_scale * cubic_term) * square)) + 0.5
    value = v * half
    slope = half + (value * (1.0 - half)) * (
        2.0 * tanh_scale + (6.0 * tanh_scale * cubic_term) * square
    )
    return value, slope


def dot(a, b, contract=((1,), (0,))):
    return lax.dot_general(a, b, (contract, ((), ())), preferred_element_type=F32)


NT = ((1,), (1,))
TN = ((0,), (0,))


def each_peer(me, act):
    for first, last, unroll in ((16, PEERS, 4), (1, 16, 5)):

        @pl.loop(first, last, unroll=unroll)
        def _(i):
            act(lax.rem(me + i, PEERS))


def kernel(
    count_ref,
    gain_ref,
    bias_ref,
    df1_ref,
    uf1_ref,
    df2_ref,
    uf2_ref,
    series_hbm,
    taps_hbm,
    up1_hbm,
    down1_hbm,
    up2_hbm,
    down2_hbm,
    upstream_hbm,
    m_recv,
    total_out,
    series,
    taps,
    up1,
    down1,
    up2,
    down2,
    upstream,
    padded,
    packed_taps,
    conv,
    rows32,
    normed_ref,
    low_t,
    slope_ref,
    u_send,
    u_recv,
    f_send,
    f_recv,
    g_send,
    g_recv,
    m_send,
    st_send,
    st_recv,
    dft,
    ufr,
    gh_ref,
    hid_ref,
    gp2_ref,
    back_ref,
    part,
    part_recv,
    total,
    total_recv,
    load_sems,
    self_sems,
    sends,
    arrivals,
):
    me = lax.axis_index("var")
    limit = count_ref[0]
    live_rows = limit - me * SENSORS

    def remote(src, dst, ssem, rsem, peer):
        return pltpu.make_async_remote_copy(
            src_ref=src,
            dst_ref=dst,
            send_sem=ssem,
            recv_sem=rsem,
            device_id={"var": peer},
            device_id_type=MESH,
        )

    loads = [
        pltpu.make_async_copy(src, dst, load_sems.at[i])
        for i, (src, dst) in enumerate(
            (
                (upstream_hbm, upstream),
                (series_hbm, series),
                (taps_hbm, taps),
                (up1_hbm, up1),
                (down1_hbm, down1),
                (down2_hbm, down2),
                (up2_hbm, up2),
            )
        )
    ]
    for load in loads:
        load.start()

    barrier = pltpu.get_barrier_semaphore()

    def greet(peer):
        pl.semaphore_signal(barrier, inc=1, device_id={"var": peer}, device_id_type=MESH)

    each_peer(me, greet)

    loads[0].wait()
    row_index = lax.broadcasted_iota(jnp.int32, (SENSORS, PATCHES), 0)
    live_sensor = (row_index < live_rows).astype(F32)

    @pl.loop(0, SENSORS, unroll=8)
    def _(m):
        rows32[pl.ds(m, CHANNELS, stride=SENSORS), :] = upstream[m].astype(F32)

    @pl.loop(0, CHANNELS, unroll=8)
    def _(d):
        at = pl.multiple_of(d * SENSORS, SENSORS)
        u_send[d] = (rows32[pl.ds(at, SENSORS), :] * live_sensor).astype(BF16)

    df1 = df1_ref[...].astype(F32)
    zero8 = jnp.zeros((8, CHANNELS), F32)
    dft[...] = jnp.concatenate(
        [
            jnp.concatenate([df1, zero8], axis=1),
            jnp.concatenate([zero8, df1], axis=1),
            jnp.zeros((112, 128), F32),
        ],
        axis=0,
    ).astype(BF16)
    uf1_32 = uf1_ref[...].astype(F32)
    ufr[0] = jnp.concatenate([uf1_32, jnp.zeros((120, HIDDEN), F32)], axis=0).astype(BF16)
    ufr[1] = jnp.concatenate(
        [jnp.zeros((8, HIDDEN), F32), uf1_32, jnp.zeros((112, HIDDEN), F32)], axis=0
    ).astype(BF16)

    loads[1].wait()
    loads[2].wait()
    padded[:, 0 : HALF * 8, :] = jnp.zeros((GROUPS, HALF * 8, 128), F32)
    padded[:, (HALF + PATCHES) * 8 : PADDED * 8, :] = jnp.zeros((GROUPS, HALF * 8, 128), F32)

    for g in range(GROUPS):

        @pl.loop(0, 8, unroll=8)
        def _(r):
            both = jnp.concatenate(
                [series[16 * g + r].astype(F32), series[16 * g + 8 + r].astype(F32)], axis=0
            )
            padded[g, pl.ds(HALF * 8 + r, PATCHES, stride=8), :] = both.T

    @pl.loop(0, TAPS, unroll=3)
    def _(k):
        row = taps[k].astype(F32)
        for g in range(GROUPS):
            packed_taps[k, g] = jnp.concatenate(
                [row[16 * g : 16 * g + 8], row[16 * g + 8 : 16 * g + 16]], axis=1
            )

    pl.semaphore_wait(barrier, PEERS - 1)
    mine = pl.ds(pl.multiple_of(me * SENSORS, SENSORS), SENSORS)
    neighbour = lax.rem(me + 1, PEERS)

    def u_start(peer):
        remote(
            u_send.at[pl.ds(OWN * peer, OWN)], u_recv.at[:, mine, :], sends.at[0], arrivals.at[0], peer
        ).start()

    each_peer(me, u_start)
    u_self = pltpu.make_async_copy(
        u_send.at[pl.ds(OWN * me, OWN)], u_recv.at[:, mine, :], self_sems.at[0]
    )
    u_self.start()
    u_all = remote(
        u_send.at[pl.ds(0, OWN * (PEERS - 1))],
        u_recv.at[:, pl.ds(0, SENSORS * (PEERS - 1)), :],
        sends.at[0],
        arrivals.at[0],
        neighbour,
    )

    sub = lax.broadcasted_iota(jnp.int32, (8, 128), 0)
    lane = lax.broadcasted_iota(jnp.int32, (8, 128), 1)
    high = (lane >= CHANNELS).astype(jnp.int32) * 8

    def group_mask(g):
        return (sub + high + 16 * g < live_rows).astype(F32)

    def conv_group(g, sums):
        def conv_block(nb, acc_sum):
            base = pl.multiple_of(nb * (BLOCK * 8), BLOCK * 8)
            acc = [None] * BLOCK
            tap = {}
            for j in range(BLOCK + TAPS - 1):
                x = padded[g, pl.ds(base + 8 * j, 8), :]
                if j < TAPS:
                    tap[j] = packed_taps[j, g]
                for i in range(max(0, j - TAPS + 1), min(BLOCK - 1, j) + 1):
                    term = tap[j - i] * x
                    acc[i] = term if acc[i] is None else acc[i] + term
            for i in range(BLOCK):
                conv[g, pl.ds(base + 8 * i, 8), :] = acc[i]
                acc_sum = acc_sum + acc[i]
            return acc_sum

        group_sum = lax.fori_loop(0, PATCHES // BLOCK, conv_block, jnp.zeros((8, 128), F32))
        return sums + group_sum * group_mask(g)

    sums = lax.fori_loop(0, GROUPS, conv_group, jnp.zeros((8, 128), F32))

    def fold(v):
        v = jnp.sum(v, axis=0, keepdims=True)
        return v + pltpu.roll(v, CHANNELS, axis=1)

    sum_row = fold(sums)
    own_count = jnp.clip(live_rows, 0, SENSORS).astype(F32) * PATCHES
    own_mean = sum_row / jnp.maximum(own_count, 1.0)

    def square_group(g, squares):
        def block(b, acc):
            at = pl.multiple_of(b * 128, 128)
            c = conv[g, pl.ds(at, 128), :] - own_mean
            return acc + jnp.sum((c * c).reshape(16, 8, 128), axis=0)

        group = lax.fori_loop(0, 8, block, jnp.zeros((8, 128), F32))
        return squares + group * group_mask(g)

    square_row = fold(lax.fori_loop(0, GROUPS, square_group, jnp.zeros((8, 128), F32)))
    stats = jnp.where(
        sub == 0,
        sum_row,
        jnp.where(sub == 1, square_row, jnp.where(sub == 2, own_mean, own_count)),
    )
    st_send[...] = stats
    st_recv[me] = stats

    each_peer(
        me,
        lambda peer: remote(
            st_send, st_recv.at[me], sends.at[1], arrivals.at[1], peer
        ).start(),
    )

    st_many = remote(
        st_recv.at[pl.ds(0, PEERS - 1)],
        st_recv.at[pl.ds(0, PEERS - 1)],
        sends.at[1],
        arrivals.at[1],
        neighbour,
    )
    st_many.wait_recv()
    st_all = st_recv[...]
    st_sum = jnp.sum(st_all, axis=0)
    live_total = limit.astype(F32) * PATCHES
    bn_mean = st_sum[0:1] / live_total
    means = st_all[:, 2:3, :] - bn_mean[None]
    shift_squares = jnp.sum(st_all[:, 3:4, :] * means * means, axis=0)
    spread = (st_sum[1:2] + shift_squares) / live_total
    gain = jnp.concatenate([gain_ref[...], gain_ref[...]], axis=1)
    bias = jnp.concatenate([bias_ref[...], bias_ref[...]], axis=1)
    bn_scale = gain * lax.rsqrt(spread + 1e-05)

    loads[3].wait()
    loads[4].wait()
    zero_half = jnp.zeros((CHANNELS, HIDDEN), BF16)
    lane_row = lax.broadcasted_iota(jnp.int32, (1, 128), 1)
    high_row = (lane_row >= CHANNELS).astype(jnp.int32) * 8

    def f_copy(c, peer):
        return remote(
            f_send.at[c, pl.ds(OWN * peer, OWN)],
            f_recv.at[:, me, pl.ds(c * CHUNK, CHUNK), :],
            sends.at[2 + c],
            arrivals.at[2 + c],
            peer,
        )

    f_all = [
        remote(
            f_send.at[c, pl.ds(0, OWN * (PEERS - 1))],
            f_recv.at[:, pl.ds(0, PEERS - 1), pl.ds(0, CHUNK), :],
            sends.at[2 + c],
            arrivals.at[2 + c],
            neighbour,
        )
        for c in range(CHUNKS)
    ]
    f_self = []
    for c in range(CHUNKS):
        for gl in range(GROUPS // CHUNKS):
            g = c * (GROUPS // CHUNKS) + gl

            @pl.loop(0, 8, unroll=8)
            def _(r):
                pair = g * 8 + r
                live = (high_row + 16 * g + r < live_rows).astype(F32)
                centered = conv[g, pl.ds(r, PATCHES, stride=8), :] - bn_mean
                normed = ((centered * bn_scale + bias) * live).astype(BF16)
                normed_ref[pair] = normed
                low = dot(normed, dft[...], NT).astype(BF16)
                low_t[pair] = dot(dft[0:16, :], normed, NT).astype(BF16)
                lhs = jnp.concatenate([normed, low], axis=1)
                for half in range(2):
                    m = 16 * g + 8 * half + r
                    weight = up1[m]
                    rhs = jnp.concatenate(
                        [weight, zero_half, ufr[half]] if half == 0 else [zero_half, weight, ufr[half]],
                        axis=0,
                    )
                    value, slope = gelu_parts(dot(lhs, rhs))
                    slope_ref[m] = slope
                    feature = dot(down1[m], value.astype(BF16), NT)
                    rows32[pl.ds(16 * gl + 8 * half + r, CHANNELS, stride=CHUNK), :] = feature

        @pl.loop(0, CHANNELS, unroll=8)
        def _(d):
            at = pl.multiple_of(d * CHUNK, CHUNK)
            f_send[c, d] = rows32[pl.ds(at, CHUNK), :].astype(BF16)

        each_peer(me, lambda peer: f_copy(c, peer).start())

        f_self.append(
            pltpu.make_async_copy(
                f_send.at[c, pl.ds(OWN * me, OWN)],
                f_recv.at[:, me, pl.ds(c * CHUNK, CHUNK), :],
                self_sems.at[1 + c],
            )
        )
        f_self[-1].start()

    u_self.wait()
    u_all.wait_recv()

    loads[5].wait()
    loads[6].wait()
    for dd in range(OWN):
        gh_ref[dd] = dot(down2[dd], u_recv[dd]).T

    pres = tuple(jnp.zeros((PATCHES, HIDDEN), F32) for _ in range(OWN))
    for c in range(CHUNKS):
        f_self[c].wait()
        f_all[c].wait_recv()
        rows = pl.ds(c * CHUNK, CHUNK)
        many = 256 // CHUNK

        def mix(b, pres):
            at = pl.ds(b * many, many)
            return tuple(
                pre
                + dot(
                    f_recv[dd, at, rows, :].reshape(256, PATCHES),
                    up2[dd, at, rows, :].reshape(256, HIDDEN),
                    TN,
                )
                for dd, pre in enumerate(pres)
            )

        pres = lax.fori_loop(0, PEERS // many, mix, pres)

    def project(b, lows):
        at = pl.ds(pl.multiple_of(b * 256, 256), 256)
        return tuple(
            low + dot(df2_ref[:, at], f_recv[dd, pl.ds(b * 4, 4)].reshape(256, PATCHES))
            for dd, low in enumerate(lows)
        )

    lows = lax.fori_loop(
        0,
        SLOTS // 256,
        project,
        tuple(jnp.zeros((8, PATCHES), F32) for _ in range(OWN)),
        unroll=4,
    )
    for dd in range(OWN):
        pre = pres[dd]
        low = lows[dd].astype(BF16)
        value, slope = gelu_parts(pre + dot(low, uf2_ref[...], TN))
        hid_ref[dd] = value.astype(BF16)
        gp2 = (gh_ref[dd] * slope).astype(BF16)
        gp2_ref[dd] = gp2
        back_ref[dd] = dot(uf2_ref[...], gp2, NT).astype(BF16)
        gu2 = dot(low, gp2)
        for t in range(2):
            tile = gu2[:, 128 * t : 128 * (t + 1)]
            part[16 + t] = tile if dd == 0 else part[16 + t] + tile

    own_block = pl.ds(OWN * me, OWN)

    def g_copy(half, peer):
        return remote(
            g_send.at[half, peer],
            g_recv.at[half, own_block],
            sends.at[6 + half],
            arrivals.at[6 + half],
            peer,
        )

    def m_copy(peer):
        return remote(m_send.at[peer], m_recv.at[own_block], sends.at[8], arrivals.at[8], peer)

    g_all = [
        remote(
            g_send.at[half, pl.ds(0, PEERS - 1)],
            g_send.at[half, pl.ds(0, PEERS - 1)],
            sends.at[6 + half],
            arrivals.at[6 + half],
            neighbour,
        )
        for half in range(HALVES)
    ]
    m_all = remote(
        m_send.at[pl.ds(0, PEERS - 1)],
        m_send.at[pl.ds(0, PEERS - 1)],
        sends.at[8],
        arrivals.at[8],
        neighbour,
    )
    g_self = [
        pltpu.make_async_copy(
            g_send.at[half, me], g_recv.at[half, own_block], self_sems.at[5 + half]
        )
        for half in range(HALVES)
    ]
    m_self = pltpu.make_async_copy(m_send.at[me], m_recv.at[own_block], self_sems.at[7])

    own_chip = me // 2
    sibling = 2 * own_chip + 1 - lax.rem(me, 2)

    def chip_at(i):
        return lax.rem(own_chip + 1 + lax.rem(i + 7, 15), 16)

    def each_chip(act, send):
        @pl.loop(0, 5)
        def _(q):
            chips = [chip_at(3 * q + i) for i in range(3)]
            if act is not None:
                for chip in chips:
                    act(chip)
            for chip in chips:
                send(2 * chip)
                send(2 * chip + 1)

        if act is not None:
            act(own_chip)
        send(sibling)

    def g_block(chip):
        at = pl.ds(pl.multiple_of(chip * 128, 128), 128)
        gd2 = []
        for dd in range(OWN):
            grad = dot(up2[dd, pl.ds(2 * chip, 2)].reshape(128, HIDDEN), gp2_ref[dd], NT) + dot(df2_ref[:, at], back_ref[dd], TN)
            gd2.append(
                dot(back_ref[dd], f_recv[dd, pl.ds(2 * chip, 2)].reshape(128, PATCHES), NT)
            )
            grad = grad.astype(BF16)
            for part_of in range(4):
                core, half = part_of // 2, part_of % 2
                g_send[half, 2 * chip + core, dd] = grad[BATCH * part_of : BATCH * (part_of + 1)]
        part[chip] = gd2[0] + gd2[1]

    def m_block(chip):
        at = pl.ds(pl.multiple_of(chip * 128, 128), 128)
        for dd in range(OWN):
            mix_t = dot(hid_ref[dd], down2[dd, :, at]).T.astype(BF16)
            m_send[2 * chip, dd] = mix_t[0:SENSORS]
            m_send[2 * chip + 1, dd] = mix_t[SENSORS:]

    each_chip(g_block, lambda peer: g_copy(0, peer).start())
    each_chip(None, lambda peer: g_copy(1, peer).start())
    for half in range(HALVES):
        g_self[half].start()

    def tiles(n, ref, at):
        return remote(
            ref.at[pl.ds(0, n)], ref.at[pl.ds(0, n)], sends.at[at], arrivals.at[at], neighbour
        )

    def is_owner(device, first, last):
        return jnp.logical_and(device >= first, device < last)

    def to_owners(first, last, at):
        @pl.loop(first, last)
        def _(owner):
            @pl.when(owner != me)
            def _():
                remote(
                    part.at[owner], part_recv.at[me], sends.at[at], arrivals.at[at], owner
                ).start()

        @pl.when(is_owner(me, first, last))
        def _():
            part_recv[me] = part[me]

    def from_owners(first, last, at):
        @pl.when(is_owner(me, first, last))
        def _():
            tiles(PEERS - 1, part_recv, at).wait_recv()
            summed = jnp.sum(part_recv[...], axis=0)
            total[...] = summed
            total_recv[me] = summed
            each_peer(
                me,
                lambda peer: remote(
                    total, total_recv.at[me], sends.at[at + 1], arrivals.at[at + 1], peer
                ).start(),
            )

    def by_role(first, last, owner_act, other_act):
        owner = is_owner(me, first, last)
        pl.when(owner)(owner_act)
        pl.when(jnp.logical_not(owner))(other_act)

    def totals_arrive(first, last, at):
        by_role(
            first,
            last,
            lambda: tiles(last - first - 1, total_recv, at + 1).wait_recv(),
            lambda: tiles(last - first, total_recv, at + 1).wait_recv(),
        )

    def totals_left(first, last, at):
        def owner_act():
            tiles(last - first - 1, part, at).wait_send()
            tiles(PEERS - 1, total_recv, at + 1).wait_send()

        by_role(first, last, owner_act, lambda: tiles(last - first, part, at).wait_send())

    to_owners(0, 18, 9)

    each_chip(m_block, lambda peer: m_copy(peer).start())
    m_self.start()

    gu1 = jnp.zeros((8, HIDDEN), F32)
    gd1 = jnp.zeros((16, 128), F32)
    for g in range(GROUPS):
        half_of = g // 2
        if g == 2:
            from_owners(0, 18, 9)
        if g % 2 == 0:
            g_self[half_of].wait()
            g_all[half_of].wait_recv()

            @pl.loop(0, CHANNELS, unroll=8)
            def _(d):
                at = pl.multiple_of(d * BATCH, BATCH)
                rows32[pl.ds(at, BATCH), :] = g_recv[half_of, d].astype(F32)

        def back(r, carry):
            gu1, gd1 = carry
            pair = g * 8 + r
            grad = jnp.concatenate(
                [
                    rows32[pl.ds(16 * (g % 2) + 8 * half + r, CHANNELS, stride=BATCH), :]
                    for half in range(2)
                ],
                axis=0,
            ).T.astype(BF16)
            gps, backs = [], []
            for half in range(2):
                m = 16 * g + 8 * half + r
                weight = down1[m]
                rhs = jnp.concatenate(
                    [weight, zero_half] if half == 0 else [zero_half, weight], axis=0
                )
                gp = (dot(grad, rhs) * slope_ref[m]).astype(BF16)
                gps.append(gp)
                backs.append(dot(uf1_ref[...], gp, NT))
            low = low_t[pair].astype(F32)
            lhs = jnp.concatenate([low[0:8], low[8:16]], axis=1).astype(BF16)
            gu1 = gu1 + dot(lhs, jnp.concatenate(gps, axis=0))
            gd1 = gd1 + dot(jnp.concatenate(backs, axis=0).astype(BF16), normed_ref[pair])
            return gu1, gd1

        gu1, gd1 = lax.fori_loop(0, 8, back, (gu1, gd1), unroll=8)

    part[18] = gu1[:, 0:128]
    part[19] = gu1[:, 128:256]
    part[20] = jnp.where(lane < CHANNELS, gd1[0:8], gd1[8:16])

    to_owners(18, TILES, 11)
    from_owners(18, TILES, 11)
    totals_arrive(0, 18, 9)
    totals_arrive(18, TILES, 11)
    total_out[...] = total_recv[0:TILES]

    m_self.wait()
    m_all.wait_recv()
    u_all.wait_send()
    st_many.wait_send()
    for sent in f_all + g_all + [m_all]:
        sent.wait_send()

    totals_left(0, 18, 9)
    totals_left(18, TILES, 11)


def finish(
    count_ref,
    series_hbm,
    received_hbm,
    total_hbm,
    mixed_hbm,
    gd1_ref,
    gu1_ref,
    gd2_ref,
    gu2_ref,
    series,
    received,
    total,
    mixed,
    rows32,
    load_sems,
    store_sems,
):
    steps = SENSORS // STEP
    loads = [
        pltpu.make_async_copy(
            received_hbm.at[:, pl.ds(step * STEP, STEP), :], received.at[step], load_sems.at[step]
        )
        for step in range(steps)
    ]
    loads.append(pltpu.make_async_copy(total_hbm, total, load_sems.at[steps]))
    blocks = [pl.ds(step * STEP, STEP) for step in range(steps)]
    series_loads = [
        pltpu.make_async_copy(
            series_hbm.at[blocks[step]], series.at[blocks[step]], load_sems.at[steps + 1 + step]
        )
        for step in range(steps)
    ]
    for step in range(steps):
        loads[step].start()
        series_loads[step].start()
    loads[steps].start()
    live_rows = count_ref[0] - lax.axis_index("var") * SENSORS
    row = lax.broadcasted_iota(jnp.int32, (STEP, PATCHES), 0)
    stores = []
    for step in range(steps):
        loads[step].wait()
        series_loads[step].wait()
        live = (row + step * STEP < live_rows).astype(F32)

        @pl.loop(0, CHANNELS, unroll=16)
        def _(d):
            rows32[pl.ds(pl.multiple_of(d * STEP, STEP), STEP), :] = (
                received[step, d].astype(F32) * live
            )

        @pl.loop(0, STEP, unroll=8)
        def _(m):
            mixed[step * STEP + m] = (
                series[step * STEP + m].astype(F32) + rows32[pl.ds(m, CHANNELS, stride=STEP), :]
            ).astype(BF16)

        stores.append(
            pltpu.make_async_copy(
                mixed.at[blocks[step]], mixed_hbm.at[blocks[step]], store_sems.at[step]
            )
        )
        stores[-1].start()

    loads[steps].wait()
    for t in range(16):
        gd2_ref[:, 128 * t : 128 * (t + 1)] = total[t]
    for t in range(2):
        gu2_ref[:, 128 * t : 128 * (t + 1)] = total[16 + t]
        gu1_ref[:, 128 * t : 128 * (t + 1)] = total[18 + t]
    both = total[20]
    gd1_ref[...] = (both + pltpu.roll(both, CHANNELS, axis=1))[:, 0:CHANNELS]
    for store in stores:
        store.wait()


def body(
    series,
    sensor_total_count,
    depthwise_weight,
    batchnorm_gain,
    batchnorm_bias,
    channel_up_weight,
    channel_down_weight,
    down_factor1,
    up_factor1,
    sensor_up_weight,
    sensor_down_weight,
    down_factor2,
    up_factor2,
    upstream,
):
    vmem = pl.BlockSpec(memory_space=pltpu.VMEM)
    hbm = pl.BlockSpec(memory_space=pltpu.HBM)
    rows = PATCHES * 8
    dma = pltpu.SemaphoreType.DMA
    received, total = pl.pallas_call(
        kernel,
        out_shape=(
            jax.ShapeDtypeStruct((CHANNELS, SENSORS, PATCHES), BF16),
            jax.ShapeDtypeStruct((TILES, 8, 128), F32),
        ),
        in_specs=[pl.BlockSpec(memory_space=pltpu.SMEM)] + [vmem] * 6 + [hbm] * 7,
        out_specs=(hbm, vmem),
        scratch_shapes=[
            pltpu.VMEM((SENSORS, CHANNELS, PATCHES), BF16),
            pltpu.VMEM((TAPS, SENSORS, CHANNELS), BF16),
            pltpu.VMEM((SENSORS, CHANNELS, HIDDEN), BF16),
            pltpu.VMEM((SENSORS, CHANNELS, HIDDEN), BF16),
            pltpu.VMEM((OWN, PEERS, SENSORS, HIDDEN), BF16),
            pltpu.VMEM((OWN, HIDDEN, SLOTS), BF16),
            pltpu.VMEM((SENSORS, CHANNELS, PATCHES), BF16),
            pltpu.VMEM((GROUPS, PADDED * 8, 128), F32),
            pltpu.VMEM((TAPS, GROUPS, 8, 128), F32),
            pltpu.VMEM((GROUPS, rows, 128), F32),
            pltpu.VMEM((SENSORS * CHANNELS, PATCHES), F32),
            pltpu.VMEM((SENSORS // 2, PATCHES, 128), BF16),
            pltpu.VMEM((SENSORS // 2, 16, PATCHES), BF16),
            pltpu.VMEM((SENSORS, PATCHES, HIDDEN), F32),
            pltpu.VMEM((CHANNELS, SENSORS, PATCHES), BF16),
            pltpu.VMEM((OWN, SLOTS, PATCHES), BF16),
            pltpu.VMEM((CHUNKS, CHANNELS, CHUNK, PATCHES), BF16),
            pltpu.VMEM((OWN, PEERS, SENSORS, PATCHES), BF16),
            pltpu.VMEM((HALVES, PEERS, OWN, BATCH, PATCHES), BF16),
            pltpu.VMEM((HALVES, CHANNELS, BATCH, PATCHES), BF16),
            pltpu.VMEM((PEERS, OWN, SENSORS, PATCHES), BF16),
            pltpu.VMEM((8, 128), F32),
            pltpu.VMEM((PEERS, 8, 128), F32),
            pltpu.VMEM((128, 128), BF16),
            pltpu.VMEM((2, 128, HIDDEN), BF16),
            pltpu.VMEM((OWN, PATCHES, HIDDEN), F32),
            pltpu.VMEM((OWN, PATCHES, HIDDEN), BF16),
            pltpu.VMEM((OWN, PATCHES, HIDDEN), BF16),
            pltpu.VMEM((OWN, 8, PATCHES), BF16),
            pltpu.VMEM((PEERS, 8, 128), F32),
            pltpu.VMEM((PEERS, 8, 128), F32),
            pltpu.VMEM((8, 128), F32),
            pltpu.VMEM((PEERS, 8, 128), F32),
            dma((7,)),
            dma((8,)),
            dma((13,)),
            dma((13,)),
        ],
        compiler_params=pltpu.CompilerParams(
            collective_id=0, has_side_effects=True, vmem_limit_bytes=60 * 1024 * 1024
        ),
        cost_estimate=pl.CostEstimate(
            flops=2_000_000_000, bytes_accessed=12_000_000, transcendentals=2_200_000
        ),
    )(
        sensor_total_count,
        batchnorm_gain.reshape(1, CHANNELS),
        batchnorm_bias.reshape(1, CHANNELS),
        down_factor1.T,
        up_factor1,
        down_factor2.T,
        up_factor2,
        series[0],
        jnp.transpose(depthwise_weight, (2, 0, 1)),
        channel_up_weight,
        jnp.transpose(channel_down_weight, (0, 2, 1)),
        sensor_up_weight.reshape(OWN, PEERS, SENSORS, HIDDEN),
        sensor_down_weight,
        upstream[0],
    )
    mixed, gd1, gu1, gd2, gu2 = pl.pallas_call(
        finish,
        out_shape=(
            jax.ShapeDtypeStruct((SENSORS, CHANNELS, PATCHES), BF16),
            jax.ShapeDtypeStruct((8, CHANNELS), F32),
            jax.ShapeDtypeStruct((8, HIDDEN), F32),
            jax.ShapeDtypeStruct((8, SLOTS), F32),
            jax.ShapeDtypeStruct((8, HIDDEN), F32),
        ),
        in_specs=[pl.BlockSpec(memory_space=pltpu.SMEM), hbm, hbm, hbm],
        out_specs=(hbm, vmem, vmem, vmem, vmem),
        scratch_shapes=[
            pltpu.VMEM((SENSORS, CHANNELS, PATCHES), BF16),
            pltpu.VMEM((SENSORS // STEP, CHANNELS, STEP, PATCHES), BF16),
            pltpu.VMEM((TILES, 8, 128), F32),
            pltpu.VMEM((SENSORS, CHANNELS, PATCHES), BF16),
            pltpu.VMEM((STEP * CHANNELS, PATCHES), F32),
            dma((2 * (SENSORS // STEP) + 1,)),
            dma((SENSORS // STEP,)),
        ],
        compiler_params=pltpu.CompilerParams(vmem_limit_bytes=60 * 1024 * 1024),
    )(sensor_total_count, series[0], received, total)
    return mixed[None], gd1.T, gu1, gd2.T, gu2


def solution(mesh):
    placed = (
        P("grp", "var", None, None),
        P("grp"),
        P("var", None, None),
        P(),
        P(),
        P("var", None, None),
        P("var", None, None),
        P(),
        P(),
        P("var", None, None),
        P("var", None, None),
        P(),
        P(),
        P("grp", "var", None, None),
    )
    return jax.shard_map(
        body,
        mesh=mesh,
        in_specs=placed,
        out_specs=(
            P("grp", "var", None, None),
            P("grp", None),
            P("grp", None),
            P("grp", None),
            P("grp", None),
        ),
        check_vma=False,
    )
```
